512 devices in a mesh: outer: 16 (over y_lo, x), inner: 32 (over z, y_hi, core).
Axes of the slice: x: 4, y: 8 (y_hi: 2, y_lo: 4; y = y_hi * 4 + y_lo), z: 8, core: 2. Of those that a mesh axis runs over, the one named last changes fastest.
Arguments:
- queries: bfloat16 [32768, 1024], P(('outer', 'inner')), may hold values from -8 to 8
- key_rows: bfloat16 [32768, 1024], P(('outer', 'inner')), may hold values from -8 to 8
- value_rows: bfloat16 [32768, 1024], P(('outer', 'inner')), may hold values from -6 to 6
Outputs:
- attended: float32 [32768, 1024], P(('outer', 'inner'))
The draws below stay inside these ranges and needn't reach their ends.
All inputs are finite; a program needn't handle non-finite values.
Results may differ from the reference program's by a relative error of at most 0.0021.
Values may be sent and summed in bfloat16 or wider, within the bound.
No kernel may reach another device: no remote copies, remote signals or barrier semaphores. Data moves between devices by JAX's collectives and lax.ppermute only.
A program may use at most 64 MiB of HBM per device.

```python
from functools import reduce
import jax
import jax.numpy as jnp
import numpy as np
from jax import lax

HEADS = 16
HEAD_DIM = 64
TOK_DEV = 64
GROUP_LEN = 2048
SEQUENCE = 32768


def draw_queries(key, part):
    shape = (SEQUENCE, HEADS * HEAD_DIM)
    base = jax.random.truncated_normal(jax.random.fold_in(key, 1), -6.0, 6.0, shape, jnp.float32)
    return base.astype(jnp.bfloat16)


def draw_key_rows(key, part):
    shape = (SEQUENCE, HEADS * HEAD_DIM)
    base = jax.random.truncated_normal(jax.random.fold_in(key, 2), -6.0, 6.0, shape, jnp.float32)
    return base.astype(jnp.bfloat16)


def block_levels(key, extent, cuts, smallest, top_value):
    def one(axis_at, blocks):
        heights = jax.random.uniform(jax.random.fold_in(jax.random.fold_in(key, 6), axis_at), (blocks,), jnp.float32, smallest / len(cuts), top_value / len(cuts))
        return jnp.repeat(jnp.exp(heights), extent[axis_at] // blocks).reshape((-1,) + (1,) * (len(extent) - axis_at - 1))

    loudness = one(*cuts[0])
    for cut in cuts[1:]:
        loudness = loudness * one(*cut)
    return loudness


def gaussian(key, shape, scale, reach, split=(), kind=jnp.bfloat16):
    gain = block_levels(key, shape, split, -0.22, 0.18) if split else 1.0
    values = jax.random.normal(key, shape, jnp.float32) * scale * gain
    return jnp.minimum(jnp.maximum(values, -reach), reach).astype(kind)


def setup_inputs(seed: int = 0) -> dict:
    key_list = jax.random.split(jax.random.key(seed), 4)
    return {
        "queries": draw_queries(jax.random.fold_in(key_list[3], 71), 0),
        "key_rows": draw_key_rows(jax.random.fold_in(key_list[3], 71), 0),
        "value_rows": gaussian(key_list[2], (SEQUENCE, HEADS * HEAD_DIM), 1.0, 6.0, ((0, 512),)),
    }


FLOOR_SCORE = -1.0e30


def dense_causal(query_rows, key_rows, value_rows, ranks):
    scale = HEAD_DIM ** -0.5
    scores = jnp.dot(query_rows.astype(jnp.float32), key_rows.astype(jnp.float32).T, precision=lax.Precision.HIGHEST) * scale
    scores = jnp.where(ranks[None, :] <= ranks[:, None], scores, FLOOR_SCORE)
    row_max = jnp.max(scores, axis=1)
    weights = jnp.exp(scores - row_max[:, None])
    denominator = jnp.sum(weights, axis=1)
    rounded = lax.optimization_barrier(weights.astype(jnp.bfloat16)).astype(jnp.float32)
    summed = jnp.dot(rounded, value_rows.astype(jnp.float32), precision=lax.Precision.HIGHEST)
    return summed / denominator[:, None], row_max + jnp.log(denominator)


def level_one(queries, key_rows, value_rows):
    blocks = SEQUENCE // TOK_DEV
    ranks = jnp.arange(TOK_DEV, dtype=jnp.int32)

    def one_block(pieces):
        return jax.vmap(dense_causal, in_axes=(1, 1, 1, None), out_axes=(1, 1))(pieces[0], pieces[1], pieces[2], ranks)

    shaped = tuple(a.reshape(blocks, TOK_DEV, HEADS, HEAD_DIM) for a in (queries, key_rows, value_rows))
    outputs, lses = lax.map(one_block, shaped)
    return outputs.reshape(SEQUENCE, HEADS, HEAD_DIM), lses.reshape(SEQUENCE, HEADS)


def level_two(queries, key_rows, value_rows):
    groups = SEQUENCE // GROUP_LEN
    class_len = GROUP_LEN // 4
    ranks = jnp.arange(class_len, dtype=jnp.int32)

    def regroup(array):
        return array.reshape(groups, class_len, 4, HEADS, HEAD_DIM).transpose(0, 3, 2, 1, 4).reshape(groups * HEADS * 4, class_len, HEAD_DIM)

    def one_item(pieces):
        return dense_causal(pieces[0], pieces[1], pieces[2], ranks)

    outputs, lses = lax.map(one_item, (regroup(queries), regroup(key_rows), regroup(value_rows)))
    outputs = outputs.reshape(groups, HEADS, 4, class_len, HEAD_DIM).transpose(0, 3, 2, 1, 4).reshape(SEQUENCE, HEADS, HEAD_DIM)
    lses = lses.reshape(groups, HEADS, 4, class_len).transpose(0, 3, 2, 1).reshape(SEQUENCE, HEADS)
    return outputs, lses


def level_three(queries, key_rows, value_rows):
    sixteenth = SEQUENCE // 16
    pick = np.array([head * 16 + (head // 4) * 4 + residue for head in range(HEADS) for residue in range(4)], np.int32)
    ranks = jnp.arange(sixteenth, dtype=jnp.int32)

    def regroup(array):
        spread = array.reshape(sixteenth, 16, HEADS, HEAD_DIM).transpose(2, 1, 0, 3).reshape(HEADS * 16, sixteenth, HEAD_DIM)
        return jnp.take(spread, pick, axis=0)

    def one_item(pieces):
        return dense_causal(pieces[0], pieces[1], pieces[2], ranks)

    outputs, lses = lax.map(one_item, (regroup(queries), regroup(key_rows), regroup(value_rows)))
    full_out = jnp.zeros((HEADS * 16, sixteenth, HEAD_DIM), jnp.float32).at[pick].set(outputs)
    full_lse = jnp.full((HEADS * 16, sixteenth), FLOOR_SCORE, jnp.float32).at[pick].set(lses)
    full_out = full_out.reshape(HEADS, 16, sixteenth, HEAD_DIM).transpose(2, 1, 0, 3).reshape(SEQUENCE, HEADS, HEAD_DIM)
    full_lse = full_lse.reshape(HEADS, 16, sixteenth).transpose(2, 1, 0).reshape(SEQUENCE, HEADS)
    return full_out, full_lse


def merge_levels(parts):
    row_max = reduce(jnp.maximum, [lse for _, lse in parts])
    weights = [jnp.exp(lse - row_max) for _, lse in parts]
    denominator = reduce(jnp.add, weights)
    summed = reduce(jnp.add, [weight[..., None] * output for weight, (output, _) in zip(weights, parts)])
    return summed / denominator[..., None], row_max + jnp.log(denominator)


def reference(queries, key_rows, value_rows):
    shaped = tuple(a.reshape(SEQUENCE, HEADS, HEAD_DIM) for a in (queries, key_rows, value_rows))
    first = level_one(*shaped)
    second = level_two(*shaped)
    third = level_three(*shaped)
    combined, _ = merge_levels([first, second, third])
    return combined.reshape(SEQUENCE, HEADS * HEAD_DIM)
```

```python
import functools

import jax
import jax.numpy as jnp
from jax import lax
from jax.experimental import pallas as pl
from jax.experimental.pallas import tpu as pltpu
from jax.sharding import PartitionSpec as P

TOK = 64
WIDTH = 64
LANES = 2 * WIDTH
PAIRS = 8
RES = 4
ROWS = TOK // RES
INNER = PAIRS * RES
OUTER = 16
CLASS = ROWS * INNER
FAR = CLASS // 4
FLOOR = -1e30
F32 = jnp.float32
BF16 = jnp.bfloat16


def dot(a, b):
    return jnp.dot(a, b, preferred_element_type=F32)


def dot_t(a, b):
    return lax.dot_general(a, b, (((1,), (1,)), ((), ())), preferred_element_type=F32)


def iota(shape, dim):
    return lax.broadcasted_iota(jnp.int32, shape, dim)


def one_hot(shape, row_of, col_of, dtype=BF16):
    return (row_of(iota(shape, 0)) == col_of(iota(shape, 1))).astype(F32).astype(dtype)


def by_class(r):
    return RES * (r % ROWS) + r // ROWS


def first_head(rows):
    return iota((rows, LANES), 1) < WIDTH


def stack_heads(q):
    left = first_head(q.shape[0])
    zero = jnp.zeros_like(q)
    return jnp.concatenate([jnp.where(left, q, zero), jnp.where(left, zero, q)], axis=0)


def side_heads(x):
    half = x.shape[0] // 2
    return jnp.where(
        first_head(half),
        jnp.broadcast_to(x[:half], (half, LANES)),
        jnp.broadcast_to(x[half:], (half, LANES)),
    )


def softmax_out(scores, values):
    top = jnp.max(scores, axis=1, keepdims=True)
    weights = jnp.exp(scores - top)
    total = jnp.sum(weights, axis=1, keepdims=True)
    summed = dot(weights.astype(BF16), values)
    return side_heads(summed / total), side_heads(top + jnp.log(total))


def pack_kernel(q_ref, k_ref, v_ref, out_ref):
    order = one_hot((TOK, TOK), by_class, lambda c: c)
    for at, ref in enumerate((q_ref, k_ref, v_ref)):
        rows = dot(order, ref[...]).astype(BF16)
        for pair in range(PAIRS):
            part = rows[:, pair * LANES : (pair + 1) * LANES]
            out_ref[pair * RES : (pair + 1) * RES, at * ROWS : (at + 1) * ROWS, :] = part.reshape(
                RES, ROWS, LANES
            )


def near_kernel(q_ref, k_ref, v_ref, out_ref, lse_ref):
    allowed = iota((2 * TOK, TOK), 1) <= iota((2 * TOK, TOK), 0) % TOK
    for pair in range(PAIRS):
        cols = slice(pair * LANES, (pair + 1) * LANES)
        q = stack_heads(q_ref[:, cols] * BF16(WIDTH**-0.5))
        scores = jnp.where(allowed, dot_t(q, k_ref[:, cols]), FLOOR)
        out_ref[:, cols], lse_ref[:, cols] = softmax_out(scores, v_ref[:, cols])


def section(ref, at):
    return ref[:, at * ROWS : (at + 1) * ROWS, :].reshape(CLASS, LANES)


def pick_kernel(place_ref, got_ref, q_ref, kv_ref):
    band = place_ref[0]
    pick = one_hot((FAR, CLASS), lambda r: 4 * r + band, lambda c: c)
    q_ref[...] = dot(pick, section(got_ref, 0)).astype(BF16)
    k = dot(pick, section(got_ref, 1)).astype(BF16)
    v = dot(pick, section(got_ref, 2)).astype(BF16)
    for to in range(OUTER):
        kv_ref[to, :FAR, :] = k
        kv_ref[to, FAR:, :] = v


def mid_kernel(got_ref, out_ref, lse_ref):
    q = section(got_ref, 0) * BF16(WIDTH**-0.5)
    k = section(got_ref, 1)
    v = section(got_ref, 2)
    block = 128
    for start in range(0, CLASS, block):
        end = start + block
        rows = stack_heads(q[start:end])
        shape = (2 * block, end)
        allowed = iota(shape, 1) <= start + iota(shape, 0) % block
        scores = jnp.where(allowed, dot_t(rows, k[:end]), FLOOR)
        out_ref[start:end, :], lse_ref[start:end, :] = softmax_out(scores, v[:end])


def far_kernel(place_ref, q_ref, kv_ref, mid_out_ref, mid_lse_ref, back_ref):
    band, group = place_ref[0], place_ref[1]
    q = stack_heads(q_ref[...] * BF16(WIDTH**-0.5))
    k = kv_ref[:, :FAR, :].reshape(OUTER * FAR, LANES)
    v = kv_ref[:, FAR:, :].reshape(OUTER * FAR, LANES)
    shape = (2 * FAR, OUTER * FAR)
    allowed = iota(shape, 1) <= group * FAR + iota(shape, 0) % FAR
    far_out, far_lse = softmax_out(jnp.where(allowed, dot_t(q, k), FLOOR), v)
    spread = one_hot((CLASS, FAR), lambda r: r, lambda c: 4 * c + band, F32)
    exact = functools.partial(
        jnp.dot, precision=lax.Precision.HIGHEST, preferred_element_type=F32
    )
    present = iota((CLASS, LANES), 0) % 4 == band
    far_out = exact(spread, far_out)
    far_lse = jnp.where(present, exact(spread, far_lse), FLOOR)
    mid_lse = mid_lse_ref[...]
    top = jnp.maximum(mid_lse, far_lse)
    mid_w, far_w = jnp.exp(mid_lse - top), jnp.exp(far_lse - top)
    total = mid_w + far_w
    out = (mid_w * mid_out_ref[...] + far_w * far_out) / total
    lse = top + jnp.log(total)
    high = lse.astype(BF16).astype(F32)
    middle = (lse - high).astype(BF16).astype(F32)
    low = lse - high - middle
    which = iota((CLASS, LANES), 1) % WIDTH // 16
    parts = jnp.where(
        which == 0, high, jnp.where(which == 1, middle, jnp.where(which == 2, low, 0.0))
    )
    back_ref[:, :ROWS, :] = out.astype(BF16).reshape(INNER, ROWS, LANES)
    back_ref[:, ROWS:, :] = parts.astype(BF16).reshape(INNER, ROWS, LANES)


def home_kernel(got_ref, near_out_ref, near_lse_ref, out_ref):
    order = one_hot((TOK, TOK), lambda r: r, by_class)
    shape = (LANES, LANES)
    row, col = iota(shape, 0), iota(shape, 1)
    gather = (row // WIDTH == col // WIDTH) & (row % 16 == 0)
    gather = gather.astype(F32).astype(BF16)
    for pair in range(PAIRS):
        cols = slice(pair * LANES, (pair + 1) * LANES)
        mine = got_ref[pair * RES : (pair + 1) * RES, :, :]
        out = dot(order, mine[:, :ROWS, :].reshape(TOK, LANES))
        parts = dot(order, mine[:, ROWS:, :].reshape(TOK, LANES)).astype(BF16)
        lse = dot(parts, gather)
        near_lse = near_lse_ref[:, cols]
        top = jnp.maximum(lse, near_lse)
        w, near_w = jnp.exp(lse - top), jnp.exp(near_lse - top)
        out_ref[:, cols] = (w * out + near_w * near_out_ref[:, cols]) / (w + near_w)


def call(kernel, outs, args, scalars=0, flops=0, exps=0):
    vmem = pl.BlockSpec(memory_space=pltpu.VMEM)
    specs = [pl.BlockSpec(memory_space=pltpu.SMEM)] * scalars + [vmem] * (len(args) - scalars)
    shapes = [jax.ShapeDtypeStruct(s, t) for s, t in outs]
    moved = sum(a.size * a.dtype.itemsize for a in args)
    moved += sum(s.size * s.dtype.itemsize for s in shapes)
    return pl.pallas_call(
        kernel,
        out_shape=shapes,
        in_specs=specs,
        out_specs=[vmem] * len(shapes),
        compiler_params=pltpu.CompilerParams(vmem_limit_bytes=40 * 2**20),
        cost_estimate=pl.CostEstimate(flops=flops, bytes_accessed=moved, transcendentals=exps),
    )(*args)


def on_device(queries, key_rows, value_rows):
    group = lax.axis_index("outer")
    place = jnp.stack([lax.axis_index("inner") // 8, group]).astype(jnp.int32)
    full = (TOK, PAIRS * LANES)
    (packed,) = call(
        pack_kernel, [((INNER, 3 * ROWS, LANES), BF16)], (queries, key_rows, value_rows)
    )
    got = lax.all_to_all(packed, "inner", 0, 0, tiled=True)
    near_out, near_lse = call(
        near_kernel,
        [(full, F32), (full, F32)],
        (queries, key_rows, value_rows),
        flops=2 * 16 * 64 * 64 * 128 * 2,
        exps=16 * 64 * 64,
    )
    far_q, far_kv = call(
        pick_kernel,
        [((FAR, LANES), BF16), ((OUTER, 2 * FAR, LANES), BF16)],
        (place, got),
        scalars=1,
    )
    all_kv = lax.all_to_all(far_kv, "outer", 0, 0, tiled=True)
    mid_out, mid_lse = call(
        mid_kernel,
        [((CLASS, LANES), F32), ((CLASS, LANES), F32)],
        (got,),
        flops=4 * 2 * 512 * 512 * 128,
        exps=2 * 512 * 512,
    )
    (back,) = call(
        far_kernel,
        [((INNER, 2 * ROWS, LANES), BF16)],
        (place, far_q, all_kv, mid_out, mid_lse),
        scalars=1,
        flops=4 * 2 * 128 * 2048 * 128,
        exps=2 * 128 * 2048,
    )
    home = lax.all_to_all(back, "inner", 0, 0, tiled=True)
    (out,) = call(home_kernel, [(full, F32)], (home, near_out, near_lse))
    return out


def solution(mesh):
    rows = P(("outer", "inner"), None)
    return jax.shard_map(
        on_device, mesh=mesh, in_specs=(rows,) * 3, out_specs=rows, check_vma=False
    )
```

```python
import functools

import jax
import jax.numpy as jnp
from jax import lax
from jax.experimental import pallas as pl
from jax.experimental.pallas import tpu as pltpu
from jax.sharding import PartitionSpec as P

TOK = 64
WIDTH = 64
LANES = 2 * WIDTH
PAIRS = 8
RES = 4
ROWS = TOK // RES
INNER = PAIRS * RES
HALF = 8
CLASS = ROWS * INNER
FAR = CLASS // 4
FLOOR = -1e30
F32 = jnp.float32
BF16 = jnp.bfloat16


def dot(a, b):
    return jnp.dot(a, b, preferred_element_type=F32)


def dot_t(a, b):
    return lax.dot_general(a, b, (((1,), (1,)), ((), ())), preferred_element_type=F32)


def iota(shape, dim):
    return lax.broadcasted_iota(jnp.int32, shape, dim)


def one_hot(shape, row_of, col_of, dtype=BF16):
    return (row_of(iota(shape, 0)) == col_of(iota(shape, 1))).astype(F32).astype(dtype)


def by_class(r):
    return RES * (r % ROWS) + r // ROWS


def first_head(rows):
    return iota((rows, LANES), 1) < WIDTH


def stack_heads(q):
    left = first_head(q.shape[0])
    zero = jnp.zeros_like(q)
    return jnp.concatenate([jnp.where(left, q, zero), jnp.where(left, zero, q)], axis=0)


def side_heads(x):
    half = x.shape[0] // 2
    return jnp.where(
        first_head(half),
        jnp.broadcast_to(x[:half], (half, LANES)),
        jnp.broadcast_to(x[half:], (half, LANES)),
    )


def softmax_out(scores, values):
    top = jnp.max(scores, axis=1, keepdims=True)
    weights = jnp.exp(scores - top)
    total = jnp.sum(weights, axis=1, keepdims=True)
    summed = dot(weights.astype(BF16), values)
    return side_heads(summed / total), side_heads(top + jnp.log(total))


def pack_kernel(q_ref, k_ref, v_ref, out_ref, held, sems):
    copies = [
        pltpu.make_async_copy(ref, held.at[at], sems.at[at])
        for at, ref in enumerate((q_ref, k_ref, v_ref))
    ]
    for copy in copies:
        copy.start()
    order = one_hot((TOK, TOK), by_class, lambda c: c)
    for at, copy in enumerate(copies):
        copy.wait()
        rows = dot(order, held[at]).astype(BF16)
        for pair in range(PAIRS):
            part = rows[:, pair * LANES : (pair + 1) * LANES]
            out_ref[pair * RES : (pair + 1) * RES, at * ROWS : (at + 1) * ROWS, :] = part.reshape(
                RES, ROWS, LANES
            )


def near_kernel(q_ref, k_ref, v_ref, out_ref, lse_ref):
    allowed = iota((2 * TOK, TOK), 1) <= iota((2 * TOK, TOK), 0) % TOK
    for pair in range(PAIRS):
        cols = slice(pair * LANES, (pair + 1) * LANES)
        q = stack_heads(q_ref[:, cols] * BF16(WIDTH**-0.5))
        scores = jnp.where(allowed, dot_t(q, k_ref[:, cols]), FLOOR)
        out_ref[:, cols], lse_ref[:, cols] = softmax_out(scores, v_ref[:, cols])


def section(ref, at):
    return ref[:, at * ROWS : (at + 1) * ROWS, :].reshape(CLASS, LANES)


def pick_kernel(place_ref, got_ref, q_ref, kv_ref):
    band = place_ref[0]
    pick = one_hot((FAR, CLASS), lambda r: 4 * r + band, lambda c: c)
    q_ref[...] = dot(pick, section(got_ref, 0)).astype(BF16)
    k = dot(pick, section(got_ref, 1)).astype(BF16)
    v = dot(pick, section(got_ref, 2)).astype(BF16)
    for to in range(HALF):
        kv_ref[to, :FAR, :] = k
        kv_ref[to, FAR:, :] = v


def mid_kernel(got_ref, out_ref, lse_ref):
    q = section(got_ref, 0) * BF16(WIDTH**-0.5)
    k = section(got_ref, 1)
    v = section(got_ref, 2)
    block = 128
    for start in range(0, CLASS, block):
        end = start + block
        rows = stack_heads(q[start:end])
        shape = (2 * block, end)
        allowed = iota(shape, 1) <= start + iota(shape, 0) % block
        scores = jnp.where(allowed, dot_t(rows, k[:end]), FLOOR)
        out_ref[start:end, :], lse_ref[start:end, :] = softmax_out(scores, v[:end])


def far_keys(kv_ref):
    keys = kv_ref[:, :FAR, :].reshape(HALF * FAR, LANES)
    return keys, kv_ref[:, FAR:, :].reshape(HALF * FAR, LANES)


def lse_part(lse, which):
    high = lse.astype(BF16).astype(F32)
    middle = (lse - high).astype(BF16).astype(F32)
    low = lse - high - middle
    return jnp.where(
        which == 0, high, jnp.where(which == 1, middle, jnp.where(which == 2, low, 0.0))
    )


def serve_kernel(q_ref, kv_ref, part_ref):
    k, v = far_keys(kv_ref)
    q = stack_heads(q_ref[...] * BF16(WIDTH**-0.5))
    scores = dot_t(q, k)
    top = jnp.max(scores, axis=1, keepdims=True)
    weights = jnp.exp(scores - top)
    total = jnp.sum(weights, axis=1, keepdims=True)
    part_ref[:FAR, :] = side_heads(dot(weights.astype(BF16), v) / total).astype(BF16)
    lse = top + jnp.log(total)
    lane = iota((FAR, LANES), 1)
    shape = (FAR, LANES)
    mine = jnp.where(
        lane % 16 < 8, jnp.broadcast_to(lse[:FAR], shape), jnp.broadcast_to(lse[FAR:], shape)
    )
    parts = lse_part(mine, lane % 8)
    lane = lane[:16]
    packed = parts[:16]
    for b in range(1, FAR // 16):
        packed = jnp.where(lane // 16 == b, parts[16 * b : 16 * b + 16], packed)
    part_ref[FAR:, :] = packed.astype(BF16)


def merge(out, lse, other_out, other_lse):
    top = jnp.maximum(lse, other_lse)
    w, other_w = jnp.exp(lse - top), jnp.exp(other_lse - top)
    total = w + other_w
    return (w * out + other_w * other_out) / total, top + jnp.log(total)


def spread_rows(band, dtype):
    return one_hot((CLASS, FAR), lambda r: r, lambda c: 4 * c + band, dtype)


def far_present(band):
    return iota((CLASS, LANES), 0) % 4 == band


def far_kernel(place_ref, q_ref, kv_ref, mid_out_ref, mid_lse_ref, out_ref, lse_ref):
    band, group = place_ref[0], place_ref[1]
    k, v = far_keys(kv_ref)
    q = stack_heads(q_ref[...] * BF16(WIDTH**-0.5))
    shape = (2 * FAR, HALF * FAR)
    allowed = iota(shape, 1) <= group % HALF * FAR + iota(shape, 0) % FAR
    far_out, far_lse = softmax_out(jnp.where(allowed, dot_t(q, k), FLOOR), v)
    exact = functools.partial(
        jnp.dot, precision=lax.Precision.HIGHEST, preferred_element_type=F32
    )
    spread = spread_rows(band, F32)
    far_lse = jnp.where(far_present(band), exact(spread, far_lse), FLOOR)
    out_ref[...], lse_ref[...] = merge(
        mid_out_ref[...], mid_lse_ref[...], exact(spread, far_out), far_lse
    )


def join_kernel(place_ref, part_ref, mid_out_ref, mid_lse_ref, back_ref):
    band, group = place_ref[0], place_ref[1]
    shape = (LANES, FAR // 16 * LANES)
    row, col = iota(shape, 0), iota(shape, 1)
    same = (row // 16 == col // LANES) & (row % 16 // 8 == col % LANES // WIDTH)
    gather = (same & (row % 8 < 3)).astype(F32).astype(BF16)
    wide = dot(part_ref[FAR:, :], gather)
    part_lse = jnp.concatenate(
        [wide[:, b * LANES : (b + 1) * LANES] for b in range(FAR // 16)], axis=0
    )
    high = part_lse.astype(BF16)
    middle = (part_lse - high.astype(F32)).astype(BF16)
    low = (part_lse - high.astype(F32) - middle.astype(F32)).astype(BF16)
    spread = spread_rows(band, BF16)
    present = far_present(band) & (group >= HALF)
    part_lse = dot(spread, high) + dot(spread, middle) + dot(spread, low)
    part_lse = jnp.where(present, part_lse, FLOOR)
    out, lse = merge(
        mid_out_ref[...], mid_lse_ref[...], dot(spread, part_ref[:FAR, :]), part_lse
    )
    parts = lse_part(lse, iota((CLASS, LANES), 1) % WIDTH // 16)
    back_ref[:, :ROWS, :] = out.astype(BF16).reshape(INNER, ROWS, LANES)
    back_ref[:, ROWS:, :] = parts.astype(BF16).reshape(INNER, ROWS, LANES)


def home_kernel(got_ref, near_out_ref, near_lse_ref, out_ref):
    order = one_hot((TOK, TOK), lambda r: r, by_class)
    shape = (LANES, LANES)
    row, col = iota(shape, 0), iota(shape, 1)
    gather = (row // WIDTH == col // WIDTH) & (row % 16 == 0)
    gather = gather.astype(F32).astype(BF16)
    for pair in range(PAIRS):
        cols = slice(pair * LANES, (pair + 1) * LANES)
        mine = got_ref[pair * RES : (pair + 1) * RES, :, :]
        out = dot(order, mine[:, :ROWS, :].reshape(TOK, LANES))
        parts = dot(order, mine[:, ROWS:, :].reshape(TOK, LANES)).astype(BF16)
        lse = dot(parts, gather)
        out_ref[:, cols] = merge(out, lse, near_out_ref[:, cols], near_lse_ref[:, cols])[0]


def call(kernel, outs, args, scalars=0, flops=0, exps=0, scratch=(), inside=pltpu.VMEM):
    vmem = pl.BlockSpec(memory_space=pltpu.VMEM)
    specs = [pl.BlockSpec(memory_space=pltpu.SMEM)] * scalars
    specs += [pl.BlockSpec(memory_space=inside)] * (len(args) - scalars)
    shapes = [jax.ShapeDtypeStruct(s, t) for s, t in outs]
    moved = sum(a.size * a.dtype.itemsize for a in args)
    moved += sum(s.size * s.dtype.itemsize for s in shapes)
    return pl.pallas_call(
        kernel,
        out_shape=shapes,
        in_specs=specs,
        out_specs=[vmem] * len(shapes),
        scratch_shapes=scratch,
        compiler_params=pltpu.CompilerParams(vmem_limit_bytes=40 * 2**20),
        cost_estimate=pl.CostEstimate(flops=flops, bytes_accessed=moved, transcendentals=exps),
    )(*args)


def on_device(queries, key_rows, value_rows):
    group = lax.axis_index("outer")
    place = jnp.stack([lax.axis_index("inner") // 8, group]).astype(jnp.int32)
    full = (TOK, PAIRS * LANES)
    class_wide = ((CLASS, LANES), F32)
    (packed,) = call(
        pack_kernel,
        [((INNER, 3 * ROWS, LANES), BF16)],
        (queries, key_rows, value_rows),
        scratch=[pltpu.VMEM((3, *full), BF16), pltpu.SemaphoreType.DMA((3,))],
        inside=pltpu.HBM,
    )
    got = lax.all_to_all(packed, "inner", 0, 0, tiled=True)
    near_out, near_lse = call(
        near_kernel,
        [(full, F32), (full, F32)],
        (queries, key_rows, value_rows),
        flops=2 * 16 * 64 * 64 * 128 * 2,
        exps=16 * 64 * 64,
    )
    far_q, far_kv = call(
        pick_kernel,
        [((FAR, LANES), BF16), ((HALF, 2 * FAR, LANES), BF16)],
        (place, got),
        scalars=1,
    )
    halves = [list(range(HALF)), list(range(HALF, 2 * HALF))]
    half_kv = lax.all_to_all(
        far_kv, "outer", 0, 0, tiled=True, axis_index_groups=halves
    )
    their_q = lax.ppermute(far_q, "outer", [(g + HALF, g) for g in range(HALF)])
    mid_out, mid_lse = call(
        mid_kernel,
        [class_wide, class_wide],
        (got,),
        flops=4 * 2 * 512 * 512 * 128,
        exps=2 * 512 * 512,
    )
    (part,) = call(
        serve_kernel,
        [((FAR + 16, LANES), BF16)],
        (their_q, half_kv),
        flops=4 * 2 * 128 * 1024 * 128,
        exps=2 * 128 * 1024,
    )
    part = lax.ppermute(part, "outer", [(g, g + HALF) for g in range(HALF)])
    mid_out, mid_lse = call(
        far_kernel,
        [class_wide, class_wide],
        (place, far_q, half_kv, mid_out, mid_lse),
        scalars=1,
        flops=4 * 2 * 128 * 1024 * 128,
        exps=2 * 128 * 1024,
    )
    (back,) = call(
        join_kernel,
        [((INNER, 2 * ROWS, LANES), BF16)],
        (place, part, mid_out, mid_lse),
        scalars=1,
    )
    home = lax.all_to_all(back, "inner", 0, 0, tiled=True)
    (out,) = call(home_kernel, [(full, F32)], (home, near_out, near_lse))
    return out


def solution(mesh):
    rows = P(("outer", "inner"), None)
    return jax.shard_map(
        on_device, mesh=mesh, in_specs=(rows,) * 3, out_specs=rows, check_vma=False
    )
```

```python
import jax
import jax.numpy as jnp
from jax import lax
from jax.experimental import pallas as pl
from jax.experimental.pallas import tpu as pltpu
from jax.sharding import PartitionSpec as P

TOK = 64
WIDTH = 64
LANES = 2 * WIDTH
PAIRS = 8
RES = 4
ROWS = TOK // RES
EIGHT = ROWS // 2
INNER = PAIRS * RES
HALF = 8
FOLD = 2
CHUNK = ROWS + EIGHT
CLASS = ROWS * INNER
FAR = CLASS // 4
FLOOR = -1e30
F32 = jnp.float32
BF16 = jnp.bfloat16


def dot(a, b):
    return jnp.dot(a, b, preferred_element_type=F32)


def dot_t(a, b):
    return lax.dot_general(a, b, (((1,), (1,)), ((), ())), preferred_element_type=F32)


def iota(shape, dim):
    return lax.broadcasted_iota(jnp.int32, shape, dim)


def one_hot(shape, row_of, col_of):
    return (row_of(iota(shape, 0)) == col_of(iota(shape, 1))).astype(F32).astype(BF16)


def by_class(r):
    return RES * (r % ROWS) + r // ROWS


def by_half(r):
    return RES * (r // (TOK // 2) * EIGHT + r % EIGHT) + r // EIGHT % RES


def left(shape):
    return iota(shape, len(shape) - 1) < WIDTH


def swap(x):
    return pltpu.roll(x, WIDTH, x.ndim - 1)


def beside(a, b):
    return jnp.where(left(a.shape), a, swap(b))


def beside_right(a, b):
    return jnp.where(left(a.shape), swap(a), b)


def merge(out, lse, other_out, other_lse):
    top = jnp.maximum(lse, other_lse)
    w, other_w = jnp.exp(lse - top), jnp.exp(other_lse - top)
    total = w + other_w
    return (w * out + other_w * other_out) / total, top + jnp.log(total)


def pack_kernel(q_ref, k_ref, v_ref, out_ref, held, sems):
    copies = [
        pltpu.make_async_copy(ref, held.at[at], sems.at[at])
        for at, ref in enumerate((q_ref, k_ref, v_ref))
    ]
    for copy in copies:
        copy.start()
    order = one_hot((TOK, TOK), by_class, lambda c: c)
    sorted_rows = []
    for at, copy in enumerate(copies):
        copy.wait()
        sorted_rows.append(dot(order, held[at]))
    for pair in range(PAIRS):
        cols = slice(pair * LANES, (pair + 1) * LANES)
        q, k, v = (x[:, cols] for x in sorted_rows)
        q = q.reshape(RES, ROWS, LANES)
        for head, join in enumerate((beside, beside_right)):
            kv = join(k, v).reshape(RES, ROWS, LANES)
            chunk = jnp.concatenate([kv, join(q[:, :EIGHT], q[:, EIGHT:])], axis=1)
            at = head * INNER + pair * RES
            out_ref[at : at + RES, :, :] = chunk.astype(BF16)


def near_kernel(q_ref, k_ref, v_ref, out_ref, lse_ref):
    allowed = iota((2 * TOK, TOK), 1) <= iota((2 * TOK, TOK), 0) % TOK
    mine = left((TOK, LANES))
    for pair in range(PAIRS):
        cols = slice(pair * LANES, (pair + 1) * LANES)
        q = q_ref[:, cols] * BF16(WIDTH**-0.5)
        zero = jnp.zeros_like(q)
        q = jnp.concatenate([jnp.where(mine, q, zero), jnp.where(mine, zero, q)], axis=0)
        scores = jnp.where(allowed, dot_t(q, k_ref[:, cols]), FLOOR)
        out, lse = softmax_out(scores, v_ref[:, cols])
        lse = jnp.broadcast_to(lse, out.shape)
        out_ref[:, cols] = jnp.where(mine, out[:TOK], out[TOK:])
        lse_ref[:, cols] = jnp.where(mine, lse[:TOK], lse[TOK:])


def softmax_out(scores, values):
    top = jnp.max(scores, axis=1, keepdims=True)
    weights = jnp.exp(scores - top)
    total = jnp.sum(weights, axis=1, keepdims=True)
    return dot(weights.astype(BF16), values) / total, top + jnp.log(total)


def lse_beside_out(scores, kv):
    out, lse = softmax_out(scores, kv)
    return jnp.where(left(out.shape), jnp.broadcast_to(lse, out.shape), out)


def unpack(got_ref, group):
    chunk = got_ref[group * INNER : (group + 1) * INNER, :, :].astype(F32)
    kv = chunk[:, :ROWS, :].reshape(CLASS, LANES).astype(BF16)
    packed = chunk[:, ROWS:, :] * WIDTH**-0.5
    q = jnp.concatenate([packed, swap(packed)], axis=1)
    q = jnp.where(left(q.shape), q, 0.0)
    return q.reshape(CLASS, LANES).astype(BF16), kv


def pick_kernel(place_ref, got_ref, q_ref, kv_ref):
    band = place_ref[0]
    pick = one_hot((FAR, CLASS), lambda r: 4 * r + band, lambda c: c)
    for group in range(FOLD):
        q, kv = unpack(got_ref, group)
        rows = slice(group * FAR, (group + 1) * FAR)
        q_ref[rows, :] = dot(pick, q).astype(BF16)
        far_kv = dot(pick, kv).astype(BF16)
        for to in range(HALF):
            kv_ref[to, rows, :] = far_kv


def mid_kernel(got_ref, state_ref):
    block = 128
    for group in range(FOLD):
        q, kv = unpack(got_ref, group)
        for start in range(0, CLASS, block):
            end = start + block
            shape = (block, end)
            allowed = iota(shape, 1) <= start + iota(shape, 0)
            scores = jnp.where(allowed, dot_t(q[start:end], kv[:end]), FLOOR)
            at = group * CLASS + start
            state_ref[at : at + block, :] = lse_beside_out(scores, kv[:end])


def far_kernel(place_ref, q_ref, kv_ref, mid_ref, back_ref):
    band, group = place_ref[0], place_ref[1]
    first = kv_ref[:, :FAR, :].reshape(HALF * FAR, LANES)
    second = kv_ref[:, FAR:, :].reshape(HALF * FAR, LANES)
    shape = (FAR, HALF * FAR)
    allowed = iota(shape, 1) <= group * FAR + iota(shape, 0)
    over_first = dot_t(q_ref[...], first)
    over_second = jnp.where(allowed, dot_t(q_ref[FAR:, :], second), FLOOR)
    early = lse_beside_out(jnp.where(allowed, over_first[:FAR], FLOOR), first)
    late = lse_beside_out(
        jnp.concatenate([over_first[FAR:], over_second], axis=1),
        jnp.concatenate([first, second], axis=0),
    )
    spread = one_hot((CLASS, FAR), lambda r: r, lambda c: 4 * c + band)
    present = iota((CLASS, LANES), 0) % 4 == band
    for at, far in enumerate((early, late)):
        high = far.astype(BF16)
        rest = far - high.astype(F32)
        middle = rest.astype(BF16)
        low = (rest - middle.astype(F32)).astype(BF16)
        far = dot(spread, high) + dot(spread, middle) + dot(spread, low)
        mid = mid_ref[at * CLASS : (at + 1) * CLASS, :]
        far_lse = jnp.where(present, swap(far), FLOOR)
        out, lse = merge(mid, swap(mid), far, far_lse)
        high = lse.astype(BF16).astype(F32)
        middle = (lse - high).astype(BF16).astype(F32)
        which = iota(lse.shape, 1) % WIDTH // 16
        parts = jnp.where(which == 1, middle, jnp.where(which == 2, lse - high - middle, 0.0))
        parts = jnp.where(which == 0, high, parts)
        chunks = []
        for x in (out, parts):
            x = x.reshape(INNER, ROWS, LANES)
            chunks.append(beside_right(x[:, :EIGHT], x[:, EIGHT:]))
        back_ref[at * INNER : (at + 1) * INNER, :, :] = jnp.concatenate(chunks, axis=1).astype(BF16)


def home_kernel(got_ref, near_out_ref, near_lse_ref, out_ref):
    order = one_hot((TOK, TOK), lambda r: r, by_half)
    shape = (LANES, LANES)
    row, col = iota(shape, 0), iota(shape, 1)
    gather = (row // WIDTH == col // WIDTH) & (row % 16 == 0)
    gather = gather.astype(F32).astype(BF16)
    for pair in range(PAIRS):
        cols = slice(pair * LANES, (pair + 1) * LANES)
        rows = slice(pair * RES, (pair + 1) * RES)
        a = got_ref[rows, :, :].astype(F32)
        b = got_ref[INNER + pair * RES : INNER + (pair + 1) * RES, :, :].astype(F32)
        both = jnp.concatenate([beside(a, b), beside_right(a, b)], axis=0).astype(F32)
        tall = (TOK, LANES)
        out = dot(order, both[:, :EIGHT, :].reshape(tall).astype(BF16))
        parts = dot(order, both[:, EIGHT:, :].reshape(tall).astype(BF16)).astype(BF16)
        lse = dot(parts, gather)
        out_ref[:, cols] = merge(out, lse, near_out_ref[:, cols], near_lse_ref[:, cols])[0]


def call(kernel, outs, args, scalars=0, flops=0, exps=0, scratch=(), inside=pltpu.VMEM, mib=40):
    vmem = pl.BlockSpec(memory_space=pltpu.VMEM)
    specs = [pl.BlockSpec(memory_space=pltpu.SMEM)] * scalars
    specs += [pl.BlockSpec(memory_space=inside)] * (len(args) - scalars)
    shapes = [jax.ShapeDtypeStruct(s, t) for s, t in outs]
    moved = sum(a.size * a.dtype.itemsize for a in args)
    moved += sum(s.size * s.dtype.itemsize for s in shapes)
    return pl.pallas_call(
        kernel,
        out_shape=shapes,
        in_specs=specs,
        out_specs=[vmem] * len(shapes),
        scratch_shapes=scratch,
        compiler_params=pltpu.CompilerParams(vmem_limit_bytes=mib * 2**20),
        cost_estimate=pl.CostEstimate(flops=flops, bytes_accessed=moved, transcendentals=exps),
    )(*args)


def on_device(queries, key_rows, value_rows):
    group = lax.axis_index("outer") % HALF
    place = jnp.stack([lax.axis_index("inner") // 8, group]).astype(jnp.int32)
    full = (TOK, PAIRS * LANES)
    folded = [
        [(g + HALF * half) * INNER + i for half in range(FOLD) for i in range(INNER)]
        for g in range(HALF)
    ]
    halves = [list(range(half * HALF, (half + 1) * HALF)) for half in range(FOLD)]
    (packed,) = call(
        pack_kernel,
        [((FOLD * INNER, CHUNK, LANES), BF16)],
        (queries, key_rows, value_rows),
        scratch=[pltpu.VMEM((3, *full), BF16), pltpu.SemaphoreType.DMA((3,))],
        inside=pl.ANY,
        mib=60,
    )
    got = lax.all_to_all(
        packed, ("outer", "inner"), 0, 0, tiled=True, axis_index_groups=folded
    )
    near_out, near_lse = call(
        near_kernel,
        [(full, F32), (full, F32)],
        (queries, key_rows, value_rows),
        flops=2 * 16 * 64 * 64 * 128 * 2,
        exps=16 * 64 * 64,
    )
    far_q, far_kv = call(
        pick_kernel,
        [((FOLD * FAR, LANES), BF16), ((HALF, FOLD * FAR, LANES), BF16)],
        (place, got),
        scalars=1,
    )
    all_kv = lax.all_to_all(far_kv, "outer", 0, 0, tiled=True, axis_index_groups=halves)
    (mid,) = call(
        mid_kernel,
        [((FOLD * CLASS, LANES), F32)],
        (got,),
        flops=4 * 2 * 512 * 512 * 128,
        exps=2 * 512 * 512,
    )
    (back,) = call(
        far_kernel,
        [((FOLD * INNER, ROWS, LANES), BF16)],
        (place, far_q, all_kv, mid),
        scalars=1,
        flops=4 * 3 * 128 * 1024 * 128,
        exps=3 * 128 * 1024,
    )
    home = lax.all_to_all(
        back, ("outer", "inner"), 0, 0, tiled=True, axis_index_groups=folded
    )
    (out,) = call(home_kernel, [(full, F32)], (home, near_out, near_lse))
    return out


def solution(mesh):
    rows = P(("outer", "inner"), None)
    return jax.shard_map(
        on_device, mesh=mesh, in_specs=(rows,) * 3, out_specs=rows, check_vma=False
    )
```

```python
import jax
import jax.numpy as jnp
from jax import lax
from jax.experimental import pallas as pl
from jax.experimental.pallas import tpu as pltpu
from jax.sharding import PartitionSpec as P

TOK = 64
WIDTH = 64
LANES = 2 * WIDTH
PAIRS = 8
RES = 4
ROWS = TOK // RES
EIGHT = ROWS // 2
INNER = PAIRS * RES
HALF = 8
FOLD = 2
CHUNK = ROWS + EIGHT
CLASS = ROWS * INNER
FAR = CLASS // 4
FLOOR = -1e30
F32 = jnp.float32
BF16 = jnp.bfloat16


def dot(a, b):
    return jnp.dot(a, b, preferred_element_type=F32)


def dot_t(a, b):
    return lax.dot_general(a, b, (((1,), (1,)), ((), ())), preferred_element_type=F32)


def iota(shape, dim):
    return lax.broadcasted_iota(jnp.int32, shape, dim)


def one_hot(shape, row_of, col_of):
    return (row_of(iota(shape, 0)) == col_of(iota(shape, 1))).astype(F32).astype(BF16)


def by_class(r):
    return RES * (r % ROWS) + r // ROWS


def by_half(r):
    return RES * (r // (TOK // 2) * EIGHT + r % EIGHT) + r // EIGHT % RES


def left(shape):
    return iota(shape, len(shape) - 1) < WIDTH


def swap(x):
    return pltpu.roll(x, WIDTH, x.ndim - 1)


def beside(a, b):
    return jnp.where(left(a.shape), a, swap(b))


def beside_right(a, b):
    return jnp.where(left(a.shape), swap(a), b)


def merge(out, lse, other_out, other_lse):
    top = jnp.maximum(lse, other_lse)
    w, other_w = jnp.exp(lse - top), jnp.exp(other_lse - top)
    total = w + other_w
    return (w * out + other_w * other_out) / total, top + jnp.log(total)


def pack_kernel(q_ref, k_ref, v_ref, out_ref, held, chunks, in_sems, out_sems):
    copies = [
        pltpu.make_async_copy(ref, held.at[at], in_sems.at[at])
        for at, ref in enumerate((k_ref, v_ref, q_ref))
    ]
    for copy in copies:
        copy.start()
    order = one_hot((TOK, TOK), by_class, lambda c: c)
    sorted_rows = []
    for at, copy in enumerate(copies):
        copy.wait()
        sorted_rows.append(dot(order, held[at]))
    sends = []
    for pair in range(PAIRS):
        cols = slice(pair * LANES, (pair + 1) * LANES)
        k, v, q = (x[:, cols] for x in sorted_rows)
        q = q.reshape(RES, ROWS, LANES)
        for head, join in enumerate((beside, beside_right)):
            kv = join(k, v).reshape(RES, ROWS, LANES)
            chunk = jnp.concatenate([kv, join(q[:, :EIGHT], q[:, EIGHT:])], axis=1)
            rows = pl.ds(head * INNER + pair * RES, RES)
            chunks[rows, :, :] = chunk.astype(BF16)
            sends.append(
                pltpu.make_async_copy(
                    chunks.at[rows], out_ref.at[rows], out_sems.at[len(sends)]
                )
            )
            sends[-1].start()
    for send in sends:
        send.wait()


def near_kernel(q_ref, k_ref, v_ref, out_ref, lse_ref):
    allowed = iota((2 * TOK, TOK), 1) <= iota((2 * TOK, TOK), 0) % TOK
    mine = left((TOK, LANES))
    for pair in range(PAIRS):
        cols = slice(pair * LANES, (pair + 1) * LANES)
        q = q_ref[:, cols] * BF16(WIDTH**-0.5)
        zero = jnp.zeros_like(q)
        q = jnp.concatenate([jnp.where(mine, q, zero), jnp.where(mine, zero, q)], axis=0)
        scores = jnp.where(allowed, dot_t(q, k_ref[:, cols]), FLOOR)
        out, lse = softmax_out(scores, v_ref[:, cols])
        lse = jnp.broadcast_to(lse, out.shape)
        out_ref[:, cols] = jnp.where(mine, out[:TOK], out[TOK:])
        lse_ref[:, cols] = jnp.where(mine, lse[:TOK], lse[TOK:])


def softmax_out(scores, values):
    top = jnp.max(scores, axis=1, keepdims=True)
    weights = jnp.exp(scores - top)
    total = jnp.sum(weights, axis=1, keepdims=True)
    return dot(weights.astype(BF16), values) / total, top + jnp.log(total)


def keys_values(got_ref, group):
    return got_ref[group * INNER : (group + 1) * INNER, :ROWS, :].reshape(CLASS, LANES)


def scaled_queries(got_ref, group):
    packed = got_ref[group * INNER : (group + 1) * INNER, ROWS:, :].astype(F32) * WIDTH**-0.5
    q = jnp.concatenate([packed, swap(packed)], axis=1)
    q = jnp.where(left(q.shape), q, 0.0)
    return q.reshape(CLASS, LANES).astype(BF16)


def far_rows(band):
    return one_hot(
        (FAR, CLASS), lambda r: r % INNER * ROWS + r // INNER * 4 + band, lambda c: c
    )


def far_rank(n):
    return n // FAR * FAR + n % INNER * 4 + n % FAR // INNER


def lse_parts(lse):
    high = lse.astype(BF16).astype(F32)
    middle = (lse - high).astype(BF16).astype(F32)
    which = iota(lse.shape, 1) % WIDTH // 16
    parts = jnp.where(which == 1, middle, jnp.where(which == 2, lse - high - middle, 0.0))
    return jnp.where(which == 0, high, parts)


def pick_kernel(place_ref, got_ref, kv_ref, held, sems):
    pick = far_rows(place_ref[0])
    sends = []
    for group in range(FOLD):
        rows = pl.ds(group * FAR, FAR)
        held[rows, :] = dot(pick, keys_values(got_ref, group)).astype(BF16)
        for to in range(HALF):
            sends.append(
                pltpu.make_async_copy(
                    held.at[rows], kv_ref.at[to, rows], sems.at[len(sends)]
                )
            )
            sends[-1].start()
    for send in sends:
        send.wait()


def mid_kernel(place_ref, got_ref, far_q_ref, state_ref, base_ref):
    pick = far_rows(place_ref[0])
    block = 128
    for group in range(FOLD):
        q, kv = scaled_queries(got_ref, group), keys_values(got_ref, group)
        far_q_ref[group * FAR : (group + 1) * FAR, :] = dot(pick, q).astype(BF16)
        for start in range(0, CLASS, block):
            end = start + block
            shape = (block, end)
            allowed = iota(shape, 1) <= start + iota(shape, 0)
            scores = jnp.where(allowed, dot_t(q[start:end], kv[:end]), FLOOR)
            out, lse = softmax_out(scores, kv[:end])
            lse = jnp.broadcast_to(lse, out.shape)
            at = group * CLASS + start
            state_ref[at : at + block, :] = jnp.where(left(out.shape), lse, out)
            packed = []
            for x in (out, lse_parts(lse)):
                x = x.reshape(block // ROWS, ROWS, LANES)
                packed.append(beside_right(x[:, :EIGHT], x[:, EIGHT:]))
            packed = jnp.concatenate(packed, axis=1)
            base_ref[at : at + block, :] = packed.reshape(block, LANES)


def far_kernel(place_ref, q_ref, kv_ref, state_ref, base_ref, back_ref, fresh):
    band, group = place_ref[0], place_ref[1]
    first = kv_ref[:, :FAR, :].reshape(HALF * FAR, LANES)
    second = kv_ref[:, FAR:, :].reshape(HALF * FAR, LANES)
    shape = (FAR, HALF * FAR)
    allowed = far_rank(iota(shape, 1)) <= group * FAR + far_rank(iota(shape, 0))
    over_first = dot_t(q_ref[...], first)
    over_second = jnp.where(allowed, dot_t(q_ref[FAR:, :], second), FLOOR)
    early = softmax_out(jnp.where(allowed, over_first[:FAR], FLOOR), first)
    late = softmax_out(
        jnp.concatenate([over_first[FAR:], over_second], axis=1),
        jnp.concatenate([first, second], axis=0),
    )
    for at, (far_out, far_lse) in enumerate((early, late)):
        start = at * CLASS + band
        mid = jnp.concatenate(
            [state_ref[pl.ds(start + 4 * lot, INNER, stride=ROWS), :] for lot in range(4)], axis=0
        )
        out, lse = merge(mid, swap(mid), far_out, jnp.broadcast_to(far_lse, far_out.shape))
        for x, down in ((out, 0), (lse_parts(lse), EIGHT)):
            for lot in range(2):
                upper = x[lot * INNER : (lot + 1) * INNER]
                lower = x[(lot + 2) * INNER : (lot + 3) * INNER]
                rows = pl.ds(start + down + 4 * lot, INNER, stride=ROWS)
                fresh[rows, :] = beside_right(upper, lower)
    shape = (FOLD * CLASS, LANES)
    back = jnp.where(iota(shape, 0) % 4 == band, fresh[: FOLD * CLASS, :], base_ref[...])
    back_ref[...] = back.astype(BF16).reshape(FOLD * INNER, ROWS, LANES)


def home_kernel(got_ref, near_out_ref, near_lse_ref, out_ref, held, sems):
    order = one_hot((TOK, TOK), lambda r: r, by_half)
    shape = (LANES, LANES)
    row, col = iota(shape, 0), iota(shape, 1)
    gather = (row // WIDTH == col // WIDTH) & (row % 16 == 0)
    gather = gather.astype(F32).astype(BF16)
    sends = []
    for pair in range(PAIRS):
        cols = slice(pair * LANES, (pair + 1) * LANES)
        rows = slice(pair * RES, (pair + 1) * RES)
        a = got_ref[rows, :, :].astype(F32)
        b = got_ref[INNER + pair * RES : INNER + (pair + 1) * RES, :, :].astype(F32)
        both = jnp.concatenate([beside(a, b), beside_right(a, b)], axis=0)
        tall = (TOK, LANES)
        out = dot(order, both[:, :EIGHT, :].reshape(tall).astype(BF16))
        parts = dot(order, both[:, EIGHT:, :].reshape(tall).astype(BF16)).astype(BF16)
        lse = dot(parts, gather)
        held[:, cols] = merge(out, lse, near_out_ref[:, cols], near_lse_ref[:, cols])[0]
        sends.append(
            pltpu.make_async_copy(held.at[:, cols], out_ref.at[:, cols], sems.at[pair])
        )
        sends[-1].start()
    for send in sends:
        send.wait()


def call(
    kernel, outs, args, scalars=0, flops=0, exps=0, scratch=(), inside=None, outside=None, mib=40
):
    vmem = pltpu.VMEM
    specs = [pl.BlockSpec(memory_space=pltpu.SMEM)] * scalars
    specs += [pl.BlockSpec(memory_space=inside or vmem)] * (len(args) - scalars)
    shapes = [jax.ShapeDtypeStruct(s, t) for s, t in outs]
    moved = sum(a.size * a.dtype.itemsize for a in args)
    moved += sum(s.size * s.dtype.itemsize for s in shapes)
    return pl.pallas_call(
        kernel,
        out_shape=shapes,
        in_specs=specs,
        out_specs=[pl.BlockSpec(memory_space=outside or vmem)] * len(shapes),
        scratch_shapes=scratch,
        compiler_params=pltpu.CompilerParams(vmem_limit_bytes=mib * 2**20),
        cost_estimate=pl.CostEstimate(flops=flops, bytes_accessed=moved, transcendentals=exps),
    )(*args)


def on_device(queries, key_rows, value_rows):
    group = lax.axis_index("outer") % HALF
    place = jnp.stack([lax.axis_index("inner") // 8, group]).astype(jnp.int32)
    full = (TOK, PAIRS * LANES)
    tall = (FOLD * CLASS, LANES)
    spare = (FOLD * CLASS + ROWS, LANES)
    dma = pltpu.SemaphoreType.DMA
    folded = [
        [(g + HALF * half) * INNER + i for half in range(FOLD) for i in range(INNER)]
        for g in range(HALF)
    ]
    halves = [list(range(half * HALF, (half + 1) * HALF)) for half in range(FOLD)]
    chunks = (FOLD * INNER, CHUNK, LANES)
    (packed,) = call(
        pack_kernel,
        [(chunks, BF16)],
        (queries, key_rows, value_rows),
        scratch=[
            pltpu.VMEM((3, *full), BF16),
            pltpu.VMEM(chunks, BF16),
            dma((3,)),
            dma((2 * PAIRS,)),
        ],
        inside=pl.ANY,
        outside=pl.ANY,
        mib=60,
    )
    got = lax.all_to_all(
        packed, ("outer", "inner"), 0, 0, tiled=True, axis_index_groups=folded
    )
    near_out, near_lse = call(
        near_kernel,
        [(full, F32), (full, F32)],
        (queries, key_rows, value_rows),
        flops=2 * 16 * 64 * 64 * 128 * 2,
        exps=16 * 64 * 64,
    )
    (far_kv,) = call(
        pick_kernel,
        [((HALF, FOLD * FAR, LANES), BF16)],
        (place, got),
        scalars=1,
        scratch=[pltpu.VMEM((FOLD * FAR, LANES), BF16), dma((FOLD * HALF,))],
        outside=pl.ANY,
    )
    all_kv = lax.all_to_all(far_kv, "outer", 0, 0, tiled=True, axis_index_groups=halves)
    far_q, state, base = call(
        mid_kernel,
        [((FOLD * FAR, LANES), BF16), (spare, F32), (tall, F32)],
        (place, got),
        scalars=1,
        flops=4 * 2 * 512 * 512 * 128,
        exps=2 * 512 * 512,
    )
    (back,) = call(
        far_kernel,
        [((FOLD * INNER, ROWS, LANES), BF16)],
        (place, far_q, all_kv, state, base),
        scalars=1,
        flops=4 * 3 * 128 * 1024 * 128,
        exps=3 * 128 * 1024,
        scratch=[pltpu.VMEM(spare, F32)],
    )
    home = lax.all_to_all(
        back, ("outer", "inner"), 0, 0, tiled=True, axis_index_groups=folded
    )
    (out,) = call(
        home_kernel,
        [(full, F32)],
        (home, near_out, near_lse),
        scratch=[pltpu.VMEM(full, F32), dma((PAIRS,))],
        outside=pl.ANY,
    )
    return out


def solution(mesh):
    rows = P(("outer", "inner"), None)
    return jax.shard_map(
        on_device, mesh=mesh, in_specs=(rows,) * 3, out_specs=rows, check_vma=False
    )
```

```python
import jax
import jax.numpy as jnp
from jax import lax
from jax.experimental import pallas as pl
from jax.experimental.pallas import tpu as pltpu
from jax.sharding import PartitionSpec as P

TOK = 64
WIDTH = 64
LANES = 2 * WIDTH
PAIRS = 8
RES = 4
ROWS = TOK // RES
EIGHT = ROWS // 2
INNER = PAIRS * RES
HALF = 8
FOLD = 2
CHUNK = ROWS + EIGHT
CLASS = ROWS * INNER
FAR = CLASS // 4
FLOOR = -1e30
F32 = jnp.float32
BF16 = jnp.bfloat16


def dot(a, b):
    return jnp.dot(a, b, preferred_element_type=F32)


def dot_t(a, b):
    return lax.dot_general(a, b, (((1,), (1,)), ((), ())), preferred_element_type=F32)


def iota(shape, dim):
    return lax.broadcasted_iota(jnp.int32, shape, dim)


def one_hot(shape, row_of, col_of):
    return (row_of(iota(shape, 0)) == col_of(iota(shape, 1))).astype(F32).astype(BF16)


def by_class(r):
    return RES * (r % ROWS) + r // ROWS


def by_half(r):
    return RES * (r // (TOK // 2) * EIGHT + r % EIGHT) + r // EIGHT % RES


def left(shape):
    return iota(shape, len(shape) - 1) < WIDTH


def swap(x):
    return pltpu.roll(x, WIDTH, x.ndim - 1)


def beside(a, b):
    return jnp.where(left(a.shape), a, swap(b))


def beside_right(a, b):
    return jnp.where(left(a.shape), swap(a), b)


def merge(out, lse, other_out, other_lse):
    top = jnp.maximum(lse, other_lse)
    w, other_w = jnp.exp(lse - top), jnp.exp(other_lse - top)
    total = w + other_w
    return (w * out + other_w * other_out) / total, top + jnp.log(total)


def copies_in(refs, held, sems):
    copies = [
        pltpu.make_async_copy(ref, held.at[at], sems.at[at]) for at, ref in enumerate(refs)
    ]
    for copy in copies:
        copy.start()
    return copies


def pack_kernel(place_ref, q_ref, k_ref, v_ref, out_ref, held, sems):
    copies = copies_in((k_ref, v_ref, q_ref), held, sems)
    order = one_hot((TOK, TOK), by_class, lambda c: c)
    sorted_rows = []
    for at, copy in enumerate(copies):
        copy.wait()
        sorted_rows.append(dot(order, held[at]))
    for pair in range(PAIRS):
        cols = slice(pair * LANES, (pair + 1) * LANES)
        k, v, q = (x[:, cols] for x in sorted_rows)
        q = q.reshape(RES, ROWS, LANES)
        for head, join in enumerate((beside, beside_right)):
            kv = join(k, v).reshape(RES, ROWS, LANES)
            chunk = jnp.concatenate([kv, join(q[:, :EIGHT], q[:, EIGHT:])], axis=1)
            at = head * INNER + pair * RES
            out_ref[at : at + RES, :, :] = chunk.astype(BF16)


def near_level(q_ref, k_ref, v_ref, out_ref, lse_ref):
    allowed = iota((2 * TOK, TOK), 1) <= iota((2 * TOK, TOK), 0) % TOK
    mine = left((TOK, LANES))
    for pair in range(PAIRS):
        cols = slice(pair * LANES, (pair + 1) * LANES)
        q = q_ref[:, cols] * BF16(WIDTH**-0.5)
        zero = jnp.zeros_like(q)
        q = jnp.concatenate([jnp.where(mine, q, zero), jnp.where(mine, zero, q)], axis=0)
        scores = jnp.where(allowed, dot_t(q, k_ref[:, cols]), FLOOR)
        out, lse = softmax_out(scores, v_ref[:, cols])
        lse = jnp.broadcast_to(lse, out.shape)
        out_ref[:, cols] = jnp.where(mine, out[:TOK], out[TOK:])
        lse_ref[:, cols] = jnp.where(mine, lse[:TOK], lse[TOK:])


def softmax_out(scores, values):
    top = jnp.max(scores, axis=1, keepdims=True)
    weights = jnp.exp(scores - top)
    total = jnp.sum(weights, axis=1, keepdims=True)
    return dot(weights.astype(BF16), values) / total, top + jnp.log(total)


def keys_values(got_ref, group):
    return got_ref[group * INNER : (group + 1) * INNER, :ROWS, :].reshape(CLASS, LANES)


def scaled_queries(got_ref, group):
    packed = got_ref[group * INNER : (group + 1) * INNER, ROWS:, :].astype(F32) * WIDTH**-0.5
    q = jnp.concatenate([packed, swap(packed)], axis=1)
    q = jnp.where(left(q.shape), q, 0.0)
    return q.reshape(CLASS, LANES).astype(BF16)


def far_rows(band):
    return one_hot(
        (FAR, CLASS), lambda r: r % INNER * ROWS + r // INNER * 4 + band, lambda c: c
    )


def far_rank(n):
    return n // FAR * FAR + n % INNER * 4 + n % FAR // INNER


def lse_parts(lse):
    high = lse.astype(BF16).astype(F32)
    middle = (lse - high).astype(BF16).astype(F32)
    which = iota(lse.shape, 1) % WIDTH // 16
    parts = jnp.where(which == 1, middle, jnp.where(which == 2, lse - high - middle, 0.0))
    return jnp.where(which == 0, high, parts)


def pick_kernel(place_ref, got_ref, kv_ref, held, sems):
    pick = far_rows(place_ref[0])
    sends = []
    for group in range(FOLD):
        rows = pl.ds(group * FAR, FAR)
        held[rows, :] = dot(pick, keys_values(got_ref, group)).astype(BF16)
        for to in range(HALF):
            sends.append(
                pltpu.make_async_copy(
                    held.at[rows], kv_ref.at[to, rows], sems.at[len(sends)]
                )
            )
            sends[-1].start()
    for send in sends:
        send.wait()


def mid_kernel(
    place_ref,
    got_ref,
    q_ref,
    k_ref,
    v_ref,
    far_q_ref,
    state_ref,
    base_ref,
    near_out_ref,
    near_lse_ref,
    held,
    sems,
):
    copies = copies_in((q_ref, k_ref, v_ref), held, sems)
    pick = far_rows(place_ref[0])
    block = 128
    for group in range(FOLD):
        q, kv = scaled_queries(got_ref, group), keys_values(got_ref, group)
        far_q_ref[group * FAR : (group + 1) * FAR, :] = dot(pick, q).astype(BF16)
        for start in range(0, CLASS, block):
            end = start + block
            shape = (block, end)
            allowed = iota(shape, 1) <= start + iota(shape, 0)
            scores = jnp.where(allowed, dot_t(q[start:end], kv[:end]), FLOOR)
            out, lse = softmax_out(scores, kv[:end])
            lse = jnp.broadcast_to(lse, out.shape)
            at = group * CLASS + start
            state_ref[at : at + block, :] = jnp.where(left(out.shape), lse, out)
            packed = []
            for x in (out, lse_parts(lse)):
                x = x.reshape(block // ROWS, ROWS, LANES)
                packed.append(beside_right(x[:, :EIGHT], x[:, EIGHT:]))
            packed = jnp.concatenate(packed, axis=1)
            base_ref[at : at + block, :] = packed.reshape(block, LANES)
    for copy in copies:
        copy.wait()
    near_level(held.at[0], held.at[1], held.at[2], near_out_ref, near_lse_ref)


def far_kernel(place_ref, q_ref, kv_ref, state_ref, base_ref, back_ref, fresh):
    band, group = place_ref[0], place_ref[1]
    first = kv_ref[:, :FAR, :].reshape(HALF * FAR, LANES)
    second = kv_ref[:, FAR:, :].reshape(HALF * FAR, LANES)
    shape = (FAR, HALF * FAR)
    allowed = far_rank(iota(shape, 1)) <= group * FAR + far_rank(iota(shape, 0))
    over_first = dot_t(q_ref[...], first)
    over_second = jnp.where(allowed, dot_t(q_ref[FAR:, :], second), FLOOR)
    early = softmax_out(jnp.where(allowed, over_first[:FAR], FLOOR), first)
    late = softmax_out(
        jnp.concatenate([over_first[FAR:], over_second], axis=1),
        jnp.concatenate([first, second], axis=0),
    )
    for at, (far_out, far_lse) in enumerate((early, late)):
        start = at * CLASS + band
        mid = jnp.concatenate(
            [state_ref[pl.ds(start + 4 * lot, INNER, stride=ROWS), :] for lot in range(4)], axis=0
        )
        out, lse = merge(mid, swap(mid), far_out, jnp.broadcast_to(far_lse, far_out.shape))
        for x, down in ((out, 0), (lse_parts(lse), EIGHT)):
            for lot in range(2):
                upper = x[lot * INNER : (lot + 1) * INNER]
                lower = x[(lot + 2) * INNER : (lot + 3) * INNER]
                rows = pl.ds(start + down + 4 * lot, INNER, stride=ROWS)
                fresh[rows, :] = beside_right(upper, lower)
    shape = (FOLD * CLASS, LANES)
    back = jnp.where(iota(shape, 0) % 4 == band, fresh[: FOLD * CLASS, :], base_ref[...])
    back_ref[...] = back.astype(BF16).reshape(FOLD * INNER, ROWS, LANES)


def home_kernel(got_ref, near_out_ref, near_lse_ref, out_ref, held, sems):
    order = one_hot((TOK, TOK), lambda r: r, by_half)
    shape = (LANES, LANES)
    row, col = iota(shape, 0), iota(shape, 1)
    gather = (row // WIDTH == col // WIDTH) & (row % 16 == 0)
    gather = gather.astype(F32).astype(BF16)
    sends = []
    for pair in range(PAIRS):
        cols = slice(pair * LANES, (pair + 1) * LANES)
        rows = slice(pair * RES, (pair + 1) * RES)
        a = got_ref[rows, :, :].astype(F32)
        b = got_ref[INNER + pair * RES : INNER + (pair + 1) * RES, :, :].astype(F32)
        both = jnp.concatenate([beside(a, b), beside_right(a, b)], axis=0)
        tall = (TOK, LANES)
        out = dot(order, both[:, :EIGHT, :].reshape(tall).astype(BF16))
        parts = dot(order, both[:, EIGHT:, :].reshape(tall).astype(BF16)).astype(BF16)
        lse = dot(parts, gather)
        held[:, cols] = merge(out, lse, near_out_ref[:, cols], near_lse_ref[:, cols])[0]
        sends.append(
            pltpu.make_async_copy(held.at[:, cols], out_ref.at[:, cols], sems.at[pair])
        )
        sends[-1].start()
    for send in sends:
        send.wait()


HBM = pl.BlockSpec(memory_space=pltpu.HBM)
VMEM = pl.BlockSpec(memory_space=pltpu.VMEM)
SMEM = pl.BlockSpec(memory_space=pltpu.SMEM)


def call(kernel, ins, outs, flops=0, exps=0, scratch=(), mib=40):
    args, in_specs = [a for a, _ in ins], [s for _, s in ins]
    shapes = [space.memory_space(s, t) for s, t, space in outs]
    moved = sum(a.size * a.dtype.itemsize for a in args)
    return pl.pallas_call(
        kernel,
        out_shape=shapes,
        in_specs=in_specs,
        out_specs=[s for *_, s in outs],
        scratch_shapes=scratch,
        compiler_params=pltpu.CompilerParams(vmem_limit_bytes=mib * 2**20),
        cost_estimate=pl.CostEstimate(flops=flops, bytes_accessed=moved, transcendentals=exps),
    )(*args)


def on_device(queries, key_rows, value_rows):
    group = lax.axis_index("outer") % HALF
    place = jnp.stack([lax.axis_index("inner") // 8, group]).astype(jnp.int32)
    full = (TOK, PAIRS * LANES)
    tall = (FOLD * CLASS, LANES)
    spare = (FOLD * CLASS + ROWS, LANES)
    dma = pltpu.SemaphoreType.DMA
    folded = [
        [(g + HALF * half) * INNER + i for half in range(FOLD) for i in range(INNER)]
        for g in range(HALF)
    ]
    halves = [list(range(half * HALF, (half + 1) * HALF)) for half in range(FOLD)]
    own = [
        (pltpu.with_memory_space_constraint(x, pltpu.HBM), HBM)
        for x in (queries, key_rows, value_rows)
    ]
    held = [pltpu.VMEM((3, *full), BF16), dma((3,))]
    (packed,) = call(
        pack_kernel,
        [(place, SMEM), *own],
        [((FOLD * INNER, CHUNK, LANES), BF16, VMEM)],
        scratch=held,
    )
    got = lax.all_to_all(
        packed, ("outer", "inner"), 0, 0, tiled=True, axis_index_groups=folded
    )
    (far_kv,) = call(
        pick_kernel,
        [(place, SMEM), (got, VMEM)],
        [((HALF, FOLD * FAR, LANES), BF16, HBM)],
        scratch=[pltpu.VMEM((FOLD * FAR, LANES), BF16), dma((FOLD * HALF,))],
    )
    all_kv = lax.all_to_all(far_kv, "outer", 0, 0, tiled=True, axis_index_groups=halves)
    far_q, state, base, near_out, near_lse = call(
        mid_kernel,
        [(place, SMEM), (got, VMEM), *own],
        [
            ((FOLD * FAR, LANES), BF16, VMEM),
            (spare, F32, VMEM),
            (tall, F32, VMEM),
            (full, F32, VMEM),
            (full, F32, VMEM),
        ],
        flops=4 * 2 * 512 * 512 * 128,
        exps=2 * 512 * 512,
        scratch=held,
    )
    (back,) = call(
        far_kernel,
        [(place, SMEM), (far_q, VMEM), (all_kv, VMEM), (state, VMEM), (base, VMEM)],
        [((FOLD * INNER, ROWS, LANES), BF16, VMEM)],
        flops=4 * 3 * 128 * 1024 * 128,
        exps=3 * 128 * 1024,
        scratch=[pltpu.VMEM(spare, F32)],
    )
    home = lax.all_to_all(
        back, ("outer", "inner"), 0, 0, tiled=True, axis_index_groups=folded
    )
    (out,) = call(
        home_kernel,
        [(home, VMEM), (near_out, VMEM), (near_lse, VMEM)],
        [(full, F32, HBM)],
        scratch=[pltpu.VMEM(full, F32), dma((PAIRS,))],
    )
    return out


def solution(mesh):
    rows = P(("outer", "inner"), None)
    return jax.shard_map(
        on_device, mesh=mesh, in_specs=(rows,) * 3, out_specs=rows, check_vma=False
    )
```

```python
import jax
import jax.numpy as jnp
from jax import lax
from jax.experimental import pallas as pl
from jax.experimental.pallas import tpu as pltpu
from jax.sharding import PartitionSpec as P

TOK = 64
WIDTH = 64
LANES = 2 * WIDTH
PAIRS = 8
RES = 4
ROWS = TOK // RES
EIGHT = ROWS // 2
INNER = PAIRS * RES
HALF = 8
FOLD = 2
CHUNK = ROWS + EIGHT
CLASS = ROWS * INNER
FAR = CLASS // 4
FLOOR = -1e30
F32 = jnp.float32
BF16 = jnp.bfloat16


def dot(a, b):
    return jnp.dot(a, b, preferred_element_type=F32)


def dot_t(a, b):
    return lax.dot_general(a, b, (((1,), (1,)), ((), ())), preferred_element_type=F32)


def iota(shape, dim):
    return lax.broadcasted_iota(jnp.int32, shape, dim)


def one_hot(shape, row_of, col_of):
    return (row_of(iota(shape, 0)) == col_of(iota(shape, 1))).astype(F32).astype(BF16)


def by_class(r):
    return RES * (r % ROWS) + r // ROWS


def by_half(r):
    return RES * (r // (TOK // 2) * EIGHT + r % EIGHT) + r // EIGHT % RES


def left(shape):
    return iota(shape, len(shape) - 1) < WIDTH


def swap(x):
    return pltpu.roll(x, WIDTH, x.ndim - 1)


def beside(a, b):
    return jnp.where(left(a.shape), a, swap(b))


def beside_right(a, b):
    return jnp.where(left(a.shape), swap(a), b)


def merge(out, lse, other_out, other_lse):
    top = jnp.maximum(lse, other_lse)
    w, other_w = jnp.exp(lse - top), jnp.exp(other_lse - top)
    total = w + other_w
    return (w * out + other_w * other_out) / total, top + jnp.log(total)


def copies_in(refs, held, sems):
    copies = [
        pltpu.make_async_copy(ref, held.at[at], sems.at[at]) for at, ref in enumerate(refs)
    ]
    for copy in copies:
        copy.start()
    return copies


def pack_kernel(place_ref, q_ref, k_ref, v_ref, out_ref, held, sems):
    copies = copies_in((k_ref, v_ref, q_ref), held, sems)
    order = one_hot((TOK, TOK), by_class, lambda c: c)
    sorted_rows = []
    for at, copy in enumerate(copies):
        copy.wait()
        sorted_rows.append(dot(order, held[at]))
    for pair in range(PAIRS):
        cols = slice(pair * LANES, (pair + 1) * LANES)
        k, v, q = (x[:, cols] for x in sorted_rows)
        q = q.reshape(RES, ROWS, LANES)
        for head, join in enumerate((beside, beside_right)):
            kv = join(k, v).reshape(RES, ROWS, LANES)
            chunk = jnp.concatenate([kv, join(q[:, :EIGHT], q[:, EIGHT:])], axis=1)
            at = head * INNER + pair * RES
            out_ref[at : at + RES, :, :] = chunk.astype(BF16)


def near_level(q_ref, k_ref, v_ref, out_ref, lse_ref):
    allowed = iota((2 * TOK, TOK), 1) <= iota((2 * TOK, TOK), 0) % TOK
    mine = left((TOK, LANES))
    for pair in range(PAIRS):
        cols = slice(pair * LANES, (pair + 1) * LANES)
        q = q_ref[:, cols] * BF16(WIDTH**-0.5)
        zero = jnp.zeros_like(q)
        q = jnp.concatenate([jnp.where(mine, q, zero), jnp.where(mine, zero, q)], axis=0)
        scores = jnp.where(allowed, dot_t(q, k_ref[:, cols]), FLOOR)
        out, lse = softmax_out(scores, v_ref[:, cols])
        lse = jnp.broadcast_to(lse, out.shape)
        out_ref[:, cols] = jnp.where(mine, out[:TOK], out[TOK:])
        lse_ref[:, cols] = jnp.where(mine, lse[:TOK], lse[TOK:])


def softmax_out(scores, values):
    top = jnp.max(scores, axis=1, keepdims=True)
    weights = jnp.exp(scores - top)
    total = jnp.sum(weights, axis=1, keepdims=True)
    return dot(weights.astype(BF16), values) / total, top + jnp.log(total)


def keys_values(got_ref, group):
    return got_ref[group * INNER : (group + 1) * INNER, :ROWS, :].reshape(CLASS, LANES)


def scaled_queries(got_ref, group):
    packed = got_ref[group * INNER : (group + 1) * INNER, ROWS:, :].astype(F32) * WIDTH**-0.5
    q = jnp.concatenate([packed, swap(packed)], axis=1)
    q = jnp.where(left(q.shape), q, 0.0)
    return q.reshape(CLASS, LANES).astype(BF16)


def far_rows(band):
    return one_hot(
        (FAR, CLASS), lambda r: r % INNER * ROWS + r // INNER * 4 + band, lambda c: c
    )


def far_rank(n):
    return n // FAR * FAR + n % INNER * 4 + n % FAR // INNER


def lse_parts(lse):
    high = lse.astype(BF16).astype(F32)
    middle = (lse - high).astype(BF16).astype(F32)
    which = iota(lse.shape, 1) % WIDTH // 16
    parts = jnp.where(which == 1, middle, jnp.where(which == 2, lse - high - middle, 0.0))
    return jnp.where(which == 0, high, parts)


def pick_kernel(place_ref, got_ref, q_ref, kv_ref):
    pick = far_rows(place_ref[0])
    for group in range(FOLD):
        rows = slice(group * FAR, (group + 1) * FAR)
        kv = dot(pick, keys_values(got_ref, group)).astype(BF16)
        for to in range(HALF):
            kv_ref[to, rows, :] = kv
        q_ref[rows, :] = dot(pick, scaled_queries(got_ref, group)).astype(BF16)


def chunk_rows(out, lse):
    packed = []
    for x in (out, lse_parts(lse)):
        x = x.reshape(x.shape[0] // ROWS, ROWS, LANES)
        packed.append(beside_right(x[:, :EIGHT], x[:, EIGHT:]))
    return jnp.concatenate(packed, axis=1).reshape(out.shape)


def mid_level(got_ref, state, back):
    block = 128
    for group in range(FOLD):
        q, kv = scaled_queries(got_ref, group), keys_values(got_ref, group)
        for start in range(0, CLASS, block):
            end = start + block
            shape = (block, end)
            allowed = iota(shape, 1) <= start + iota(shape, 0)
            scores = jnp.where(allowed, dot_t(q[start:end], kv[:end]), FLOOR)
            out, lse = softmax_out(scores, kv[:end])
            lse = jnp.broadcast_to(lse, out.shape)
            at = group * CLASS + start
            state[at : at + block, :] = jnp.where(left(out.shape), lse, out)
            back[at : at + block, :] = chunk_rows(out, lse)


def far_level(band, group, q_ref, kv_ref, state, back):
    first = kv_ref[:, :FAR, :].reshape(HALF * FAR, LANES)
    second = kv_ref[:, FAR:, :].reshape(HALF * FAR, LANES)
    shape = (FAR, HALF * FAR)
    allowed = far_rank(iota(shape, 1)) <= group * FAR + far_rank(iota(shape, 0))
    over_first = dot_t(q_ref[...], first)
    over_second = jnp.where(allowed, dot_t(q_ref[FAR:, :], second), FLOOR)
    early = softmax_out(jnp.where(allowed, over_first[:FAR], FLOOR), first)
    late = softmax_out(
        jnp.concatenate([over_first[FAR:], over_second], axis=1),
        jnp.concatenate([first, second], axis=0),
    )
    for at, (far_out, far_lse) in enumerate((early, late)):
        start = at * CLASS + band
        mid = jnp.concatenate(
            [state[pl.ds(start + 4 * lot, INNER, stride=ROWS), :] for lot in range(4)], axis=0
        )
        out, lse = merge(mid, swap(mid), far_out, jnp.broadcast_to(far_lse, far_out.shape))
        for x, down in ((out, 0), (lse_parts(lse), EIGHT)):
            for lot in range(2):
                upper = x[lot * INNER : (lot + 1) * INNER]
                lower = x[(lot + 2) * INNER : (lot + 3) * INNER]
                rows = pl.ds(start + down + 4 * lot, INNER, stride=ROWS)
                back[rows, :] = beside_right(upper, lower)


def attend_kernel(
    place_ref,
    got_ref,
    far_q_ref,
    kv_ref,
    q_ref,
    k_ref,
    v_ref,
    back_ref,
    near_out_ref,
    near_lse_ref,
    held,
    sems,
    state,
    back,
):
    copies = copies_in((q_ref, k_ref, v_ref), held, sems)
    mid_level(got_ref, state, back)
    far_level(place_ref[0], place_ref[1], far_q_ref, kv_ref, state, back)
    chunks = back[: FOLD * CLASS, :].astype(BF16)
    back_ref[...] = chunks.reshape(FOLD * INNER, ROWS, LANES)
    for copy in copies:
        copy.wait()
    near_level(held.at[0], held.at[1], held.at[2], near_out_ref, near_lse_ref)


def home_kernel(got_ref, near_out_ref, near_lse_ref, out_ref, held, sems):
    order = one_hot((TOK, TOK), lambda r: r, by_half)
    shape = (LANES, LANES)
    row, col = iota(shape, 0), iota(shape, 1)
    gather = (row // WIDTH == col // WIDTH) & (row % 16 == 0)
    gather = gather.astype(F32).astype(BF16)
    sends = []
    for pair in range(PAIRS):
        cols = slice(pair * LANES, (pair + 1) * LANES)
        rows = slice(pair * RES, (pair + 1) * RES)
        a = got_ref[rows, :, :].astype(F32)
        b = got_ref[INNER + pair * RES : INNER + (pair + 1) * RES, :, :].astype(F32)
        both = jnp.concatenate([beside(a, b), beside_right(a, b)], axis=0)
        tall = (TOK, LANES)
        out = dot(order, both[:, :EIGHT, :].reshape(tall).astype(BF16))
        parts = dot(order, both[:, EIGHT:, :].reshape(tall).astype(BF16)).astype(BF16)
        lse = dot(parts, gather)
        held[:, cols] = merge(out, lse, near_out_ref[:, cols], near_lse_ref[:, cols])[0]
        sends.append(
            pltpu.make_async_copy(held.at[:, cols], out_ref.at[:, cols], sems.at[pair])
        )
        sends[-1].start()
    for send in sends:
        send.wait()


HBM = pl.BlockSpec(memory_space=pltpu.HBM)
VMEM = pl.BlockSpec(memory_space=pltpu.VMEM)
SMEM = pl.BlockSpec(memory_space=pltpu.SMEM)


def call(kernel, ins, outs, flops=0, exps=0, scratch=(), mib=40):
    args, in_specs = [a for a, _ in ins], [s for _, s in ins]
    shapes = [space.memory_space(s, t) for s, t, space in outs]
    moved = sum(a.size * a.dtype.itemsize for a in args)
    return pl.pallas_call(
        kernel,
        out_shape=shapes,
        in_specs=in_specs,
        out_specs=[s for *_, s in outs],
        scratch_shapes=scratch,
        compiler_params=pltpu.CompilerParams(vmem_limit_bytes=mib * 2**20),
        cost_estimate=pl.CostEstimate(flops=flops, bytes_accessed=moved, transcendentals=exps),
    )(*args)


def on_device(queries, key_rows, value_rows):
    group = lax.axis_index("outer") % HALF
    place = jnp.stack([lax.axis_index("inner") // 8, group]).astype(jnp.int32)
    full = (TOK, PAIRS * LANES)
    spare = (FOLD * CLASS + ROWS, LANES)
    dma = pltpu.SemaphoreType.DMA
    folded = [
        [(g + HALF * half) * INNER + i for half in range(FOLD) for i in range(INNER)]
        for g in range(HALF)
    ]
    halves = [list(range(half * HALF, (half + 1) * HALF)) for half in range(FOLD)]
    own = [
        (pltpu.with_memory_space_constraint(x, pltpu.HBM), HBM)
        for x in (queries, key_rows, value_rows)
    ]
    held = [pltpu.VMEM((3, *full), BF16), dma((3,))]
    (packed,) = call(
        pack_kernel,
        [(place, SMEM), *own],
        [((FOLD * INNER, CHUNK, LANES), BF16, VMEM)],
        scratch=held,
    )
    got = lax.all_to_all(
        packed, ("outer", "inner"), 0, 0, tiled=True, axis_index_groups=folded
    )
    far_q, far_kv = call(
        pick_kernel,
        [(place, SMEM), (got, VMEM)],
        [((FOLD * FAR, LANES), BF16, VMEM), ((HALF, FOLD * FAR, LANES), BF16, VMEM)],
    )
    all_kv = lax.all_to_all(far_kv, "outer", 0, 0, tiled=True, axis_index_groups=halves)
    back, near_out, near_lse = call(
        attend_kernel,
        [(place, SMEM), (got, VMEM), (far_q, VMEM), (all_kv, VMEM), *own],
        [
            ((FOLD * INNER, ROWS, LANES), BF16, VMEM),
            (full, F32, VMEM),
            (full, F32, VMEM),
        ],
        scratch=[*held, pltpu.VMEM(spare, F32), pltpu.VMEM(spare, F32)],
    )
    home = lax.all_to_all(
        back, ("outer", "inner"), 0, 0, tiled=True, axis_index_groups=folded
    )
    (out,) = call(
        home_kernel,
        [(home, VMEM), (near_out, VMEM), (near_lse, VMEM)],
        [(full, F32, HBM)],
        scratch=[pltpu.VMEM(full, F32), dma((PAIRS,))],
    )
    return out


def solution(mesh):
    rows = P(("outer", "inner"), None)
    return jax.shard_map(
        on_device, mesh=mesh, in_specs=(rows,) * 3, out_specs=rows, check_vma=False
    )
```

```python
import jax
import jax.numpy as jnp
from jax import lax
from jax.experimental import pallas as pl
from jax.experimental.pallas import tpu as pltpu
from jax.sharding import PartitionSpec as P

TOK = 64
WIDTH = 64
LANES = 2 * WIDTH
PAIRS = 8
RES = 4
ROWS = TOK // RES
EIGHT = ROWS // 2
INNER = PAIRS * RES
HALF = 8
FOLD = 2
CHUNK = ROWS + EIGHT
CLASS = ROWS * INNER
FAR = CLASS // 4
FLOOR = -1e30
F32 = jnp.float32
BF16 = jnp.bfloat16


def dot(a, b):
    return jnp.dot(a, b, preferred_element_type=F32)


def dot_t(a, b):
    return lax.dot_general(a, b, (((1,), (1,)), ((), ())), preferred_element_type=F32)


def iota(shape, dim):
    return lax.broadcasted_iota(jnp.int32, shape, dim)


def one_hot(shape, row_of, col_of):
    return (row_of(iota(shape, 0)) == col_of(iota(shape, 1))).astype(F32).astype(BF16)


def by_class(r):
    return RES * (r % ROWS) + r // ROWS


def by_half(r):
    return RES * (r // (TOK // 2) * EIGHT + r % EIGHT) + r // EIGHT % RES


def left(shape):
    return iota(shape, len(shape) - 1) < WIDTH


def swap(x):
    return pltpu.roll(x, WIDTH, x.ndim - 1)


def beside(a, b):
    return jnp.where(left(a.shape), a, swap(b))


def beside_right(a, b):
    return jnp.where(left(a.shape), swap(a), b)


def merge(out, lse, other_out, other_lse):
    top = jnp.maximum(lse, other_lse)
    w, other_w = jnp.exp(lse - top), jnp.exp(other_lse - top)
    total = w + other_w
    return (w * out + other_w * other_out) / total, top + jnp.log(total)


def copies_in(refs, held, sems):
    copies = [
        pltpu.make_async_copy(ref, held.at[at], sems.at[at]) for at, ref in enumerate(refs)
    ]
    for copy in copies:
        copy.start()
    return copies


def pack_kernel(q_ref, k_ref, v_ref, out_ref, held, sems):
    copies = copies_in((k_ref, v_ref, q_ref), held, sems)
    order = one_hot((TOK, TOK), by_class, lambda c: c)
    sorted_rows = []
    for at, copy in enumerate(copies):
        copy.wait()
        sorted_rows.append(dot(order, held[at]))
    for pair in range(PAIRS):
        cols = slice(pair * LANES, (pair + 1) * LANES)
        k, v, q = (x[:, cols] for x in sorted_rows)
        q = q.reshape(RES, ROWS, LANES)
        for head, join in enumerate((beside, beside_right)):
            kv = join(k, v).reshape(RES, ROWS, LANES)
            chunk = jnp.concatenate([kv, join(q[:, :EIGHT], q[:, EIGHT:])], axis=1)
            at = head * INNER + pair * RES
            out_ref[at : at + RES, :, :] = chunk.astype(BF16)


def near_level(q_ref, k_ref, v_ref, out_ref, lse_ref):
    allowed = iota((2 * TOK, TOK), 1) <= iota((2 * TOK, TOK), 0) % TOK
    mine = left((TOK, LANES))
    for pair in range(PAIRS):
        cols = slice(pair * LANES, (pair + 1) * LANES)
        q = q_ref[:, cols] * BF16(WIDTH**-0.5)
        zero = jnp.zeros_like(q)
        q = jnp.concatenate([jnp.where(mine, q, zero), jnp.where(mine, zero, q)], axis=0)
        scores = jnp.where(allowed, dot_t(q, k_ref[:, cols]), FLOOR)
        out, lse = softmax_out(scores, v_ref[:, cols])
        lse = jnp.broadcast_to(lse, out.shape)
        out_ref[:, cols] = jnp.where(mine, out[:TOK], out[TOK:])
        lse_ref[:, cols] = jnp.where(mine, lse[:TOK], lse[TOK:])


def softmax_out(scores, values):
    top = jnp.max(scores, axis=1, keepdims=True)
    weights = jnp.exp(scores - top)
    total = jnp.sum(weights, axis=1, keepdims=True)
    return dot(weights.astype(BF16), values) / total, top + jnp.log(total)


def keys_values(got_ref, group):
    return got_ref[group * INNER : (group + 1) * INNER, :ROWS, :].reshape(CLASS, LANES)


def scaled_queries(got_ref, group):
    packed = got_ref[group * INNER : (group + 1) * INNER, ROWS:, :].astype(F32) * WIDTH**-0.5
    q = jnp.concatenate([packed, swap(packed)], axis=1)
    q = jnp.where(left(q.shape), q, 0.0)
    return q.reshape(CLASS, LANES).astype(BF16)


def place():
    return lax.axis_index("inner") // (INNER // 4), lax.axis_index("outer") % HALF


def far_rows(band):
    return one_hot(
        (FAR, CLASS), lambda r: r % INNER * ROWS + r // INNER * 4 + band, lambda c: c
    )


def far_rank(n):
    return n // FAR * FAR + n % INNER * 4 + n % FAR // INNER


def lse_parts(lse):
    high = lse.astype(BF16).astype(F32)
    middle = (lse - high).astype(BF16).astype(F32)
    which = iota(lse.shape, 1) % WIDTH // 16
    parts = jnp.where(which == 1, middle, jnp.where(which == 2, lse - high - middle, 0.0))
    return jnp.where(which == 0, high, parts)


def pick_kernel(got_ref, kv_ref, held, sems):
    pick = far_rows(place()[0])
    sends = []
    for group in range(FOLD):
        rows = pl.ds(group * FAR, FAR)
        held[rows, :] = dot(pick, keys_values(got_ref, group)).astype(BF16)
        for to in range(HALF):
            sends.append(
                pltpu.make_async_copy(
                    held.at[rows], kv_ref.at[to, rows], sems.at[len(sends)]
                )
            )
            sends[-1].start()
    for send in sends:
        send.wait()


def mid_kernel(
    got_ref,
    q_ref,
    k_ref,
    v_ref,
    far_q_ref,
    state_ref,
    base_ref,
    near_out_ref,
    near_lse_ref,
    held,
    sems,
):
    copies = copies_in((q_ref, k_ref, v_ref), held, sems)
    pick = far_rows(place()[0])
    block = 128
    for group in range(FOLD):
        q, kv = scaled_queries(got_ref, group), keys_values(got_ref, group)
        far_q_ref[group * FAR : (group + 1) * FAR, :] = dot(pick, q).astype(BF16)
        for start in range(0, CLASS, block):
            end = start + block
            shape = (block, end)
            allowed = iota(shape, 1) <= start + iota(shape, 0)
            scores = jnp.where(allowed, dot_t(q[start:end], kv[:end]), FLOOR)
            out, lse = softmax_out(scores, kv[:end])
            lse = jnp.broadcast_to(lse, out.shape)
            at = group * CLASS + start
            state_ref[at : at + block, :] = jnp.where(left(out.shape), lse, out)
            packed = []
            for x in (out, lse_parts(lse)):
                x = x.reshape(block // ROWS, ROWS, LANES)
                packed.append(beside_right(x[:, :EIGHT], x[:, EIGHT:]))
            packed = jnp.concatenate(packed, axis=1)
            base_ref[at : at + block, :] = packed.reshape(block, LANES)
    for copy in copies:
        copy.wait()
    near_level(held.at[0], held.at[1], held.at[2], near_out_ref, near_lse_ref)


def far_kernel(q_ref, kv_ref, state_ref, base_ref, back_ref, fresh):
    band, group = place()
    first = kv_ref[:, :FAR, :].reshape(HALF * FAR, LANES)
    second = kv_ref[:, FAR:, :].reshape(HALF * FAR, LANES)
    shape = (FAR, HALF * FAR)
    allowed = far_rank(iota(shape, 1)) <= group * FAR + far_rank(iota(shape, 0))
    over_first = dot_t(q_ref[...], first)
    over_second = jnp.where(allowed, dot_t(q_ref[FAR:, :], second), FLOOR)
    early = softmax_out(jnp.where(allowed, over_first[:FAR], FLOOR), first)
    late = softmax_out(
        jnp.concatenate([over_first[FAR:], over_second], axis=1),
        jnp.concatenate([first, second], axis=0),
    )
    for at, (far_out, far_lse) in enumerate((early, late)):
        start = at * CLASS + band
        mid = jnp.concatenate(
            [state_ref[pl.ds(start + 4 * lot, INNER, stride=ROWS), :] for lot in range(4)], axis=0
        )
        out, lse = merge(mid, swap(mid), far_out, jnp.broadcast_to(far_lse, far_out.shape))
        for x, down in ((out, 0), (lse_parts(lse), EIGHT)):
            for lot in range(2):
                upper = x[lot * INNER : (lot + 1) * INNER]
                lower = x[(lot + 2) * INNER : (lot + 3) * INNER]
                rows = pl.ds(start + down + 4 * lot, INNER, stride=ROWS)
                fresh[rows, :] = beside_right(upper, lower)
    shape = (FOLD * CLASS, LANES)
    back = jnp.where(iota(shape, 0) % 4 == band, fresh[: FOLD * CLASS, :], base_ref[...])
    back_ref[...] = back.astype(BF16).reshape(FOLD * INNER, ROWS, LANES)


def home_kernel(got_ref, near_out_ref, near_lse_ref, out_ref, held, sems):
    order = one_hot((TOK, TOK), lambda r: r, by_half)
    shape = (LANES, LANES)
    row, col = iota(shape, 0), iota(shape, 1)
    gather = (row // WIDTH == col // WIDTH) & (row % 16 == 0)
    gather = gather.astype(F32).astype(BF16)
    sends = []
    for pair in range(PAIRS):
        cols = slice(pair * LANES, (pair + 1) * LANES)
        rows = slice(pair * RES, (pair + 1) * RES)
        a = got_ref[rows, :, :].astype(F32)
        b = got_ref[INNER + pair * RES : INNER + (pair + 1) * RES, :, :].astype(F32)
        both = jnp.concatenate([beside(a, b), beside_right(a, b)], axis=0)
        tall = (TOK, LANES)
        out = dot(order, both[:, :EIGHT, :].reshape(tall).astype(BF16))
        parts = dot(order, both[:, EIGHT:, :].reshape(tall).astype(BF16)).astype(BF16)
        lse = dot(parts, gather)
        held[:, cols] = merge(out, lse, near_out_ref[:, cols], near_lse_ref[:, cols])[0]
        sends.append(
            pltpu.make_async_copy(held.at[:, cols], out_ref.at[:, cols], sems.at[pair])
        )
        sends[-1].start()
    for send in sends:
        send.wait()


HBM = pl.BlockSpec(memory_space=pltpu.HBM)
VMEM = pl.BlockSpec(memory_space=pltpu.VMEM)


def call(kernel, ins, outs, flops=0, exps=0, scratch=(), mib=40):
    args, in_specs = [a for a, _ in ins], [s for _, s in ins]
    shapes = [space.memory_space(s, t) for s, t, space in outs]
    moved = sum(a.size * a.dtype.itemsize for a in args)
    return pl.pallas_call(
        kernel,
        out_shape=shapes,
        in_specs=in_specs,
        out_specs=[s for *_, s in outs],
        scratch_shapes=scratch,
        compiler_params=pltpu.CompilerParams(vmem_limit_bytes=mib * 2**20),
        cost_estimate=pl.CostEstimate(flops=flops, bytes_accessed=moved, transcendentals=exps),
    )(*args)


def on_device(queries, key_rows, value_rows):
    full = (TOK, PAIRS * LANES)
    tall = (FOLD * CLASS, LANES)
    spare = (FOLD * CLASS + ROWS, LANES)
    dma = pltpu.SemaphoreType.DMA
    folded = [
        [(g + HALF * half) * INNER + i for half in range(FOLD) for i in range(INNER)]
        for g in range(HALF)
    ]
    halves = [list(range(half * HALF, (half + 1) * HALF)) for half in range(FOLD)]
    own = [
        (pltpu.with_memory_space_constraint(x, pltpu.HBM), HBM)
        for x in (queries, key_rows, value_rows)
    ]
    held = [pltpu.VMEM((3, *full), BF16), dma((3,))]
    (packed,) = call(
        pack_kernel,
        [*own],
        [((FOLD * INNER, CHUNK, LANES), BF16, VMEM)],
        scratch=held,
    )
    got = lax.all_to_all(
        packed, ("outer", "inner"), 0, 0, tiled=True, axis_index_groups=folded
    )
    (far_kv,) = call(
        pick_kernel,
        [(got, VMEM)],
        [((HALF, FOLD * FAR, LANES), BF16, HBM)],
        scratch=[pltpu.VMEM((FOLD * FAR, LANES), BF16), dma((FOLD * HALF,))],
    )
    all_kv = lax.all_to_all(far_kv, "outer", 0, 0, tiled=True, axis_index_groups=halves)
    far_q, state, base, near_out, near_lse = call(
        mid_kernel,
        [(got, VMEM), *own],
        [
            ((FOLD * FAR, LANES), BF16, VMEM),
            (spare, F32, VMEM),
            (tall, F32, VMEM),
            (full, F32, VMEM),
            (full, F32, VMEM),
        ],
        flops=4 * 2 * 512 * 512 * 128,
        exps=2 * 512 * 512,
        scratch=held,
    )
    (back,) = call(
        far_kernel,
        [(far_q, VMEM), (all_kv, VMEM), (state, VMEM), (base, VMEM)],
        [((FOLD * INNER, ROWS, LANES), BF16, VMEM)],
        flops=4 * 3 * 128 * 1024 * 128,
        exps=3 * 128 * 1024,
        scratch=[pltpu.VMEM(spare, F32)],
    )
    home = lax.all_to_all(
        back, ("outer", "inner"), 0, 0, tiled=True, axis_index_groups=folded
    )
    (out,) = call(
        home_kernel,
        [(home, VMEM), (near_out, VMEM), (near_lse, VMEM)],
        [(full, F32, HBM)],
        scratch=[pltpu.VMEM(full, F32), dma((PAIRS,))],
    )
    return out


def solution(mesh):
    rows = P(("outer", "inner"), None)
    return jax.shard_map(
        on_device, mesh=mesh, in_specs=(rows,) * 3, out_specs=rows, check_vma=False
    )
```

```python
import jax
import jax.numpy as jnp
from jax import lax
from jax.experimental import pallas as pl
from jax.experimental.pallas import tpu as pltpu
from jax.sharding import PartitionSpec as P

TOK = 64
WIDTH = 64
LANES = 2 * WIDTH
PAIRS = 8
RES = 4
ROWS = TOK // RES
EIGHT = ROWS // 2
INNER = PAIRS * RES
HALF = 8
FOLD = 2
CHUNK = ROWS + EIGHT
CLASS = ROWS * INNER
FAR = CLASS // 4
FLOOR = -1e30
F32 = jnp.float32
BF16 = jnp.bfloat16


def dot(a, b):
    return jnp.dot(a, b, preferred_element_type=F32)


def dot_t(a, b):
    return lax.dot_general(a, b, (((1,), (1,)), ((), ())), preferred_element_type=F32)


def iota(shape, dim):
    return lax.broadcasted_iota(jnp.int32, shape, dim)


def one_hot(shape, row_of, col_of):
    return (row_of(iota(shape, 0)) == col_of(iota(shape, 1))).astype(F32).astype(BF16)


def by_class(r):
    return RES * (r % ROWS) + r // ROWS


def by_half(r):
    return RES * (r // (TOK // 2) * EIGHT + r % EIGHT) + r // EIGHT % RES


def left(shape):
    return iota(shape, len(shape) - 1) < WIDTH


def swap(x):
    return pltpu.roll(x, WIDTH, x.ndim - 1)


def beside(a, b):
    return jnp.where(left(a.shape), a, swap(b))


def beside_right(a, b):
    return jnp.where(left(a.shape), swap(a), b)


def merge(out, lse, other_out, other_lse):
    top = jnp.maximum(lse, other_lse)
    w, other_w = jnp.exp(lse - top), jnp.exp(other_lse - top)
    total = w + other_w
    return (w * out + other_w * other_out) / total, top + jnp.log(total)


def copies_in(refs, held, sems):
    copies = [
        pltpu.make_async_copy(ref, held.at[at], sems.at[at]) for at, ref in enumerate(refs)
    ]
    for copy in copies:
        copy.start()
    return copies


def pack_kernel(q_ref, k_ref, v_ref, out_ref, held, sems):
    copies = copies_in((k_ref, v_ref, q_ref), held, sems)
    order = one_hot((TOK, TOK), by_class, lambda c: c)
    sorted_rows = []
    for at, copy in enumerate(copies):
        copy.wait()
        sorted_rows.append(dot(order, held[at]))
    for pair in range(PAIRS):
        cols = slice(pair * LANES, (pair + 1) * LANES)
        k, v, q = (x[:, cols] for x in sorted_rows)
        q = q.reshape(RES, ROWS, LANES)
        for head, join in enumerate((beside, beside_right)):
            kv = join(k, v).reshape(RES, ROWS, LANES)
            chunk = jnp.concatenate([kv, join(q[:, :EIGHT], q[:, EIGHT:])], axis=1)
            at = head * INNER + pair * RES
            out_ref[at : at + RES, :, :] = chunk.astype(BF16)


def near_level(q_ref, k_ref, v_ref, out_ref, lse_ref):
    allowed = iota((2 * TOK, TOK), 1) <= iota((2 * TOK, TOK), 0) % TOK
    mine = left((TOK, LANES))
    for pair in range(PAIRS):
        cols = slice(pair * LANES, (pair + 1) * LANES)
        q = q_ref[:, cols] * BF16(WIDTH**-0.5)
        zero = jnp.zeros_like(q)
        q = jnp.concatenate([jnp.where(mine, q, zero), jnp.where(mine, zero, q)], axis=0)
        scores = jnp.where(allowed, dot_t(q, k_ref[:, cols]), FLOOR)
        out, lse = softmax_out(scores, v_ref[:, cols])
        lse = jnp.broadcast_to(lse, out.shape)
        out_ref[:, cols] = jnp.where(mine, out[:TOK], out[TOK:])
        lse_ref[:, cols] = jnp.where(mine, lse[:TOK], lse[TOK:])


def softmax_out(scores, values):
    top = jnp.max(scores, axis=1, keepdims=True)
    weights = jnp.exp(scores - top)
    total = jnp.sum(weights, axis=1, keepdims=True)
    return dot(weights.astype(BF16), values) / total, top + jnp.log(total)


def keys_values(got_ref, group):
    return got_ref[group * INNER : (group + 1) * INNER, :ROWS, :].reshape(CLASS, LANES)


def scaled_queries(got_ref, group):
    packed = got_ref[group * INNER : (group + 1) * INNER, ROWS:, :].astype(F32) * WIDTH**-0.5
    q = jnp.concatenate([packed, swap(packed)], axis=1)
    q = jnp.where(left(q.shape), q, 0.0)
    return q.reshape(CLASS, LANES).astype(BF16)


def place():
    return lax.axis_index("inner") // (INNER // 4), lax.axis_index("outer") % HALF


def far_rows(band):
    return one_hot(
        (FAR, CLASS), lambda r: r % INNER * ROWS + r // INNER * 4 + band, lambda c: c
    )


def far_rank(n):
    return n // FAR * FAR + n % INNER * 4 + n % FAR // INNER


def lse_parts(lse):
    high = lse.astype(BF16).astype(F32)
    middle = (lse - high).astype(BF16).astype(F32)
    which = iota(lse.shape, 1) % WIDTH // 16
    parts = jnp.where(which == 1, middle, jnp.where(which == 2, lse - high - middle, 0.0))
    return jnp.where(which == 0, high, parts)


def own_column(parts):
    keep = iota(parts.shape, 2) % 16 == 2 * iota(parts.shape, 1)
    return jnp.where(keep, parts, 0.0)


def open_chunks(chunks):
    chunks = chunks.astype(F32)
    rows = [chunks[:, at, :, :] for at in range(EIGHT // 2)]
    lse = chunks[:, EIGHT // 2, :1, :]
    rows.append(own_column(jnp.broadcast_to(lse, (lse.shape[0], EIGHT, LANES))))
    return jnp.concatenate(rows, axis=1)


def pick_kernel(got_ref, kv_ref, held, sems):
    pick = far_rows(place()[0])
    sends = []
    for group in range(FOLD):
        rows = pl.ds(group * FAR, FAR)
        held[rows, :] = dot(pick, keys_values(got_ref, group)).astype(BF16)
        for to in range(HALF):
            sends.append(
                pltpu.make_async_copy(
                    held.at[rows], kv_ref.at[to, rows], sems.at[len(sends)]
                )
            )
            sends[-1].start()
    for send in sends:
        send.wait()


def mid_kernel(
    got_ref,
    q_ref,
    k_ref,
    v_ref,
    far_q_ref,
    state_ref,
    base_ref,
    near_out_ref,
    near_lse_ref,
    held,
    sems,
):
    copies = copies_in((q_ref, k_ref, v_ref), held, sems)
    pick = far_rows(place()[0])
    block = 128
    for group in range(FOLD):
        q, kv = scaled_queries(got_ref, group), keys_values(got_ref, group)
        far_q_ref[group * FAR : (group + 1) * FAR, :] = dot(pick, q).astype(BF16)
        for start in range(0, CLASS, block):
            end = start + block
            shape = (block, end)
            allowed = iota(shape, 1) <= start + iota(shape, 0)
            scores = jnp.where(allowed, dot_t(q[start:end], kv[:end]), FLOOR)
            out, lse = softmax_out(scores, kv[:end])
            lse = jnp.broadcast_to(lse, out.shape)
            at = group * CLASS + start
            state_ref[at : at + block, :] = jnp.where(left(out.shape), lse, out)
            packed = []
            for x in (out, lse_parts(lse)):
                x = x.reshape(block // ROWS, ROWS, LANES)
                packed.append(beside_right(x[:, :EIGHT], x[:, EIGHT:]))
            packed = jnp.concatenate(packed, axis=1)
            base_ref[at : at + block, :] = packed.reshape(block, LANES)
    for copy in copies:
        copy.wait()
    near_level(held.at[0], held.at[1], held.at[2], near_out_ref, near_lse_ref)


def far_kernel(q_ref, kv_ref, state_ref, base_ref, back_ref, fresh):
    band, group = place()
    first = kv_ref[:, :FAR, :].reshape(HALF * FAR, LANES)
    second = kv_ref[:, FAR:, :].reshape(HALF * FAR, LANES)
    shape = (FAR, HALF * FAR)
    allowed = far_rank(iota(shape, 1)) <= group * FAR + far_rank(iota(shape, 0))
    over_first = dot_t(q_ref[...], first)
    over_second = jnp.where(allowed, dot_t(q_ref[FAR:, :], second), FLOOR)
    early = softmax_out(jnp.where(allowed, over_first[:FAR], FLOOR), first)
    late = softmax_out(
        jnp.concatenate([over_first[FAR:], over_second], axis=1),
        jnp.concatenate([first, second], axis=0),
    )
    for at, (far_out, far_lse) in enumerate((early, late)):
        start = at * CLASS + band
        mid = jnp.concatenate(
            [state_ref[pl.ds(start + 4 * lot, INNER, stride=ROWS), :] for lot in range(4)], axis=0
        )
        out, lse = merge(mid, swap(mid), far_out, jnp.broadcast_to(far_lse, far_out.shape))
        for x, down in ((out, 0), (lse_parts(lse), EIGHT)):
            for lot in range(2):
                upper = x[lot * INNER : (lot + 1) * INNER]
                lower = x[(lot + 2) * INNER : (lot + 3) * INNER]
                rows = pl.ds(start + down + 4 * lot, INNER, stride=ROWS)
                fresh[rows, :] = beside_right(upper, lower)
    shape = (FOLD * CLASS, LANES)
    back = jnp.where(iota(shape, 0) % 4 == band, fresh[: FOLD * CLASS, :], base_ref[...])
    back = back.reshape(FOLD * INNER, ROWS, LANES)
    for at in range(EIGHT // 2):
        back_ref[:, at, :, :] = back[:, 2 * at : 2 * at + 2, :].astype(BF16)
    lse = jnp.sum(own_column(back[:, EIGHT:, :]), axis=1, keepdims=True).astype(BF16)
    back_ref[:, EIGHT // 2, :, :] = jnp.broadcast_to(lse, (FOLD * INNER, 2, LANES))


def home_kernel(got_ref, near_out_ref, near_lse_ref, out_ref, held, sems):
    order = one_hot((TOK, TOK), lambda r: r, by_half)
    shape = (LANES, LANES)
    row, col = iota(shape, 0), iota(shape, 1)
    gather = (row // WIDTH == col // WIDTH).astype(F32).astype(BF16)
    sends = []
    for pair in range(PAIRS):
        cols = slice(pair * LANES, (pair + 1) * LANES)
        rows = slice(pair * RES, (pair + 1) * RES)
        a = open_chunks(got_ref[rows])
        b = open_chunks(got_ref[INNER + pair * RES : INNER + (pair + 1) * RES])
        both = jnp.concatenate([beside(a, b), beside_right(a, b)], axis=0)
        tall = (TOK, LANES)
        out = dot(order, both[:, :EIGHT, :].reshape(tall).astype(BF16))
        parts = dot(order, both[:, EIGHT:, :].reshape(tall).astype(BF16)).astype(BF16)
        lse = dot(parts, gather)
        held[:, cols] = merge(out, lse, near_out_ref[:, cols], near_lse_ref[:, cols])[0]
        sends.append(
            pltpu.make_async_copy(held.at[:, cols], out_ref.at[:, cols], sems.at[pair])
        )
        sends[-1].start()
    for send in sends:
        send.wait()


HBM = pl.BlockSpec(memory_space=pltpu.HBM)
VMEM = pl.BlockSpec(memory_space=pltpu.VMEM)


def call(kernel, ins, outs, flops=0, exps=0, scratch=(), mib=40):
    args, in_specs = [a for a, _ in ins], [s for _, s in ins]
    shapes = [space.memory_space(s, t) for s, t, space in outs]
    moved = sum(a.size * a.dtype.itemsize for a in args)
    return pl.pallas_call(
        kernel,
        out_shape=shapes,
        in_specs=in_specs,
        out_specs=[s for *_, s in outs],
        scratch_shapes=scratch,
        compiler_params=pltpu.CompilerParams(vmem_limit_bytes=mib * 2**20),
        cost_estimate=pl.CostEstimate(flops=flops, bytes_accessed=moved, transcendentals=exps),
    )(*args)


def on_device(queries, key_rows, value_rows):
    full = (TOK, PAIRS * LANES)
    tall = (FOLD * CLASS, LANES)
    spare = (FOLD * CLASS + ROWS, LANES)
    dma = pltpu.SemaphoreType.DMA
    folded = [
        [(g + HALF * half) * INNER + i for half in range(FOLD) for i in range(INNER)]
        for g in range(HALF)
    ]
    halves = [list(range(half * HALF, (half + 1) * HALF)) for half in range(FOLD)]
    own = [
        (pltpu.with_memory_space_constraint(x, pltpu.HBM), HBM)
        for x in (queries, key_rows, value_rows)
    ]
    held = [pltpu.VMEM((3, *full), BF16), dma((3,))]
    (packed,) = call(
        pack_kernel,
        [*own],
        [((FOLD * INNER, CHUNK, LANES), BF16, VMEM)],
        scratch=held,
    )
    got = lax.all_to_all(
        packed, ("outer", "inner"), 0, 0, tiled=True, axis_index_groups=folded
    )
    (far_kv,) = call(
        pick_kernel,
        [(got, VMEM)],
        [((HALF, FOLD * FAR, LANES), BF16, HBM)],
        scratch=[pltpu.VMEM((FOLD * FAR, LANES), BF16), dma((FOLD * HALF,))],
    )
    all_kv = lax.all_to_all(far_kv, "outer", 0, 0, tiled=True, axis_index_groups=halves)
    far_q, state, base, near_out, near_lse = call(
        mid_kernel,
        [(got, VMEM), *own],
        [
            ((FOLD * FAR, LANES), BF16, VMEM),
            (spare, F32, VMEM),
            (tall, F32, VMEM),
            (full, F32, VMEM),
            (full, F32, VMEM),
        ],
        flops=4 * 2 * 512 * 512 * 128,
        exps=2 * 512 * 512,
        scratch=held,
    )
    (back,) = call(
        far_kernel,
        [(far_q, VMEM), (all_kv, VMEM), (state, VMEM), (base, VMEM)],
        [((FOLD * INNER, EIGHT // 2 + 1, 2, LANES), BF16, VMEM)],
        flops=4 * 3 * 128 * 1024 * 128,
        exps=3 * 128 * 1024,
        scratch=[pltpu.VMEM(spare, F32)],
    )
    home = lax.all_to_all(
        back, ("outer", "inner"), 0, 0, tiled=True, axis_index_groups=folded
    )
    (out,) = call(
        home_kernel,
        [(home, VMEM), (near_out, VMEM), (near_lse, VMEM)],
        [(full, F32, HBM)],
        scratch=[pltpu.VMEM(full, F32), dma((PAIRS,))],
    )
    return out


def solution(mesh):
    rows = P(("outer", "inner"), None)
    return jax.shard_map(
        on_device, mesh=mesh, in_specs=(rows,) * 3, out_specs=rows, check_vma=False
    )
```

```python
import jax
import jax.numpy as jnp
from jax import lax
from jax.experimental import pallas as pl
from jax.experimental.pallas import tpu as pltpu
from jax.sharding import PartitionSpec as P

TOK = 64
WIDTH = 64
LANES = 2 * WIDTH
PAIRS = 8
RES = 4
ROWS = TOK // RES
EIGHT = ROWS // 2
INNER = PAIRS * RES
HALF = 8
FOLD = 2
CHUNK = ROWS + EIGHT
CLASS = ROWS * INNER
FAR = CLASS // 4
FLOOR = -1e30
F32 = jnp.float32
BF16 = jnp.bfloat16


def dot(a, b):
    return jnp.dot(a, b, preferred_element_type=F32)


def dot_t(a, b):
    return lax.dot_general(a, b, (((1,), (1,)), ((), ())), preferred_element_type=F32)


def iota(shape, dim):
    return lax.broadcasted_iota(jnp.int32, shape, dim)


def one_hot(shape, row_of, col_of):
    return (row_of(iota(shape, 0)) == col_of(iota(shape, 1))).astype(F32).astype(BF16)


def by_class(r):
    return RES * (r % ROWS) + r // ROWS


def by_half(r):
    return RES * (r // (TOK // 2) * EIGHT + r % EIGHT) + r // EIGHT % RES


def left(shape):
    return iota(shape, len(shape) - 1) < WIDTH


def swap(x):
    return pltpu.roll(x, WIDTH, x.ndim - 1)


def beside(a, b):
    return jnp.where(left(a.shape), a, swap(b))


def beside_right(a, b):
    return jnp.where(left(a.shape), swap(a), b)


def merge(out, lse, other_out, other_lse):
    top = jnp.maximum(lse, other_lse)
    w, other_w = jnp.exp(lse - top), jnp.exp(other_lse - top)
    total = w + other_w
    return (w * out + other_w * other_out) / total, top + jnp.log(total)


def copies_in(refs, held, sems):
    copies = [
        pltpu.make_async_copy(ref, held.at[at], sems.at[at]) for at, ref in enumerate(refs)
    ]
    for copy in copies:
        copy.start()
    return copies


def pack_kernel(q_ref, k_ref, v_ref, out_ref, held, sems):
    copies = copies_in((k_ref, v_ref, q_ref), held, sems)
    order = one_hot((TOK, TOK), by_class, lambda c: c)
    sorted_rows = []
    for at, copy in enumerate(copies):
        copy.wait()
        sorted_rows.append(dot(order, held[at]))
    for pair in range(PAIRS):
        cols = slice(pair * LANES, (pair + 1) * LANES)
        k, v, q = (x[:, cols] for x in sorted_rows)
        q = q.reshape(RES, ROWS, LANES)
        for head, join in enumerate((beside, beside_right)):
            kv = join(k, v).reshape(RES, ROWS, LANES)
            chunk = jnp.concatenate([kv, join(q[:, :EIGHT], q[:, EIGHT:])], axis=1)
            at = head * INNER + pair * RES
            out_ref[at : at + RES, :, :] = chunk.astype(BF16)


def near_level(q_ref, k_ref, v_ref, out_ref, lse_ref):
    allowed = iota((2 * TOK, TOK), 1) <= iota((2 * TOK, TOK), 0) % TOK
    mine = left((TOK, LANES))
    for pair in range(PAIRS):
        cols = slice(pair * LANES, (pair + 1) * LANES)
        q = q_ref[:, cols] * BF16(WIDTH**-0.5)
        zero = jnp.zeros_like(q)
        q = jnp.concatenate([jnp.where(mine, q, zero), jnp.where(mine, zero, q)], axis=0)
        scores = jnp.where(allowed, dot_t(q, k_ref[:, cols]), FLOOR)
        out, lse = softmax_out(scores, v_ref[:, cols])
        lse = jnp.broadcast_to(lse, out.shape)
        out_ref[:, cols] = jnp.where(mine, out[:TOK], out[TOK:])
        lse_ref[:, cols] = jnp.where(mine, lse[:TOK], lse[TOK:])


def softmax_out(scores, values):
    top = jnp.max(scores, axis=1, keepdims=True)
    weights = jnp.exp(scores - top)
    total = jnp.sum(weights, axis=1, keepdims=True)
    return dot(weights.astype(BF16), values) / total, top + jnp.log(total)


def keys_values(got_ref, group):
    return got_ref[group * INNER : (group + 1) * INNER, :ROWS, :].reshape(CLASS, LANES)


def scaled_queries(got_ref, group):
    packed = got_ref[group * INNER : (group + 1) * INNER, ROWS:, :].astype(F32) * WIDTH**-0.5
    q = jnp.concatenate([packed, swap(packed)], axis=1)
    q = jnp.where(left(q.shape), q, 0.0)
    return q.reshape(CLASS, LANES).astype(BF16)


def place():
    return lax.axis_index("inner") // (INNER // 4), lax.axis_index("outer") % HALF


def far_rows(band):
    return one_hot(
        (FAR, CLASS), lambda r: r % INNER * ROWS + r // INNER * 4 + band, lambda c: c
    )


def far_rank(n):
    return n // FAR * FAR + n % INNER * 4 + n % FAR // INNER


def lse_parts(lse):
    high = lse.astype(BF16).astype(F32)
    middle = (lse - high).astype(BF16).astype(F32)
    which = iota(lse.shape, 1) % WIDTH // 16
    parts = jnp.where(which == 1, middle, jnp.where(which == 2, lse - high - middle, 0.0))
    return jnp.where(which == 0, high, parts)


def own_column(parts):
    keep = iota(parts.shape, 2) % 16 == 2 * iota(parts.shape, 1)
    return jnp.where(keep, parts, 0.0)


def open_chunks(chunks):
    chunks = chunks.astype(F32)
    rows = [chunks[:, at, :, :] for at in range(EIGHT // 2)]
    lse = chunks[:, EIGHT // 2, :1, :]
    rows.append(own_column(jnp.broadcast_to(lse, (lse.shape[0], EIGHT, LANES))))
    return jnp.concatenate(rows, axis=1)


def pick_kernel(got_ref, kv_ref, held, sems):
    pick = far_rows(place()[0])
    sends = []
    for group in range(FOLD):
        rows = pl.ds(group * FAR, FAR)
        held[rows, :] = dot(pick, keys_values(got_ref, group)).astype(BF16)
        for to in range(HALF):
            sends.append(
                pltpu.make_async_copy(
                    held.at[rows], kv_ref.at[to, rows], sems.at[len(sends)]
                )
            )
            sends[-1].start()
    for send in sends:
        send.wait()


def mid_kernel(
    got_ref,
    q_ref,
    k_ref,
    v_ref,
    far_q_ref,
    state_ref,
    base_ref,
    near_out_ref,
    near_lse_ref,
    held,
    sems,
):
    copies = copies_in((q_ref, k_ref, v_ref), held, sems)
    pick = far_rows(place()[0])
    block = 128
    for group in range(FOLD):
        q, kv = scaled_queries(got_ref, group), keys_values(got_ref, group)
        far_q_ref[group * FAR : (group + 1) * FAR, :] = dot(pick, q).astype(BF16)
        for start in range(0, CLASS, block):
            end = start + block
            shape = (block, end)
            allowed = iota(shape, 1) <= start + iota(shape, 0)
            scores = jnp.where(allowed, dot_t(q[start:end], kv[:end]), FLOOR)
            out, lse = softmax_out(scores, kv[:end])
            lse = jnp.broadcast_to(lse, out.shape)
            at = group * CLASS + start
            state_ref[at : at + block, :] = jnp.where(left(out.shape), lse, out)
            packed = []
            for x in (out, lse_parts(lse)):
                x = x.reshape(block // ROWS, ROWS, LANES)
                packed.append(beside_right(x[:, :EIGHT], x[:, EIGHT:]))
            packed = jnp.concatenate([packed[0], own_column(packed[1])], axis=1)
            base_ref[at : at + block, :] = packed.reshape(block, LANES)
    for copy in copies:
        copy.wait()
    near_level(held.at[0], held.at[1], held.at[2], near_out_ref, near_lse_ref)


def far_kernel(q_ref, kv_ref, state_ref, base_ref, back_ref, fresh):
    fresh[: FOLD * CLASS, :] = base_ref[...]
    band, group = place()
    first = kv_ref[:, :FAR, :].reshape(HALF * FAR, LANES)
    second = kv_ref[:, FAR:, :].reshape(HALF * FAR, LANES)
    shape = (FAR, HALF * FAR)
    allowed = far_rank(iota(shape, 1)) <= group * FAR + far_rank(iota(shape, 0))
    over_first = dot_t(q_ref[...], first)
    over_second = jnp.where(allowed, dot_t(q_ref[FAR:, :], second), FLOOR)
    early = softmax_out(jnp.where(allowed, over_first[:FAR], FLOOR), first)
    late_first = over_first[FAR:]
    top = jnp.maximum(
        jnp.max(late_first, axis=1, keepdims=True), jnp.max(over_second, axis=1, keepdims=True)
    )
    w_first, w_second = jnp.exp(late_first - top), jnp.exp(over_second - top)
    total = jnp.sum(w_first, axis=1, keepdims=True) + jnp.sum(w_second, axis=1, keepdims=True)
    summed = dot(w_first.astype(BF16), first) + dot(w_second.astype(BF16), second)
    late = (summed / total, top + jnp.log(total))
    for at, (far_out, far_lse) in enumerate((early, late)):
        start = at * CLASS + band
        mid = jnp.concatenate(
            [state_ref[pl.ds(start + 4 * lot, INNER, stride=ROWS), :] for lot in range(4)], axis=0
        )
        out, lse = merge(mid, swap(mid), far_out, jnp.broadcast_to(far_lse, far_out.shape))
        column = iota((INNER, LANES), 1) % 16
        for x, down in ((out, 0), (lse_parts(lse), EIGHT)):
            for lot in range(2):
                upper = x[lot * INNER : (lot + 1) * INNER]
                lower = x[(lot + 2) * INNER : (lot + 3) * INNER]
                rows = beside_right(upper, lower)
                if down:
                    rows = jnp.where(column == 2 * (band + 4 * lot), rows, 0.0)
                fresh[pl.ds(start + down + 4 * lot, INNER, stride=ROWS), :] = rows
    back = fresh[: FOLD * CLASS, :].reshape(FOLD * INNER, ROWS, LANES)
    for at in range(EIGHT // 2):
        back_ref[:, at, :, :] = back[:, 2 * at : 2 * at + 2, :].astype(BF16)
    lse = jnp.sum(back[:, EIGHT:, :], axis=1, keepdims=True).astype(BF16)
    back_ref[:, EIGHT // 2, :, :] = jnp.broadcast_to(lse, (FOLD * INNER, 2, LANES))


def home_kernel(got_ref, near_out_ref, near_lse_ref, out_ref, held, sems):
    order = one_hot((TOK, TOK), lambda r: r, by_half)
    shape = (LANES, LANES)
    row, col = iota(shape, 0), iota(shape, 1)
    gather = (row // WIDTH == col // WIDTH).astype(F32).astype(BF16)
    sends = []
    for pair in range(PAIRS):
        cols = slice(pair * LANES, (pair + 1) * LANES)
        rows = slice(pair * RES, (pair + 1) * RES)
        a = open_chunks(got_ref[rows])
        b = open_chunks(got_ref[INNER + pair * RES : INNER + (pair + 1) * RES])
        both = jnp.concatenate([beside(a, b), beside_right(a, b)], axis=0)
        tall = (TOK, LANES)
        out = dot(order, both[:, :EIGHT, :].reshape(tall).astype(BF16))
        parts = dot(order, both[:, EIGHT:, :].reshape(tall).astype(BF16)).astype(BF16)
        lse = dot(parts, gather)
        held[:, cols] = merge(out, lse, near_out_ref[:, cols], near_lse_ref[:, cols])[0]
        sends.append(
            pltpu.make_async_copy(held.at[:, cols], out_ref.at[:, cols], sems.at[pair])
        )
        sends[-1].start()
    for send in sends:
        send.wait()


HBM = pl.BlockSpec(memory_space=pltpu.HBM)
VMEM = pl.BlockSpec(memory_space=pltpu.VMEM)


def call(kernel, ins, outs, flops=0, exps=0, scratch=(), mib=40):
    args, in_specs = [a for a, _ in ins], [s for _, s in ins]
    shapes = [space.memory_space(s, t) for s, t, space in outs]
    moved = sum(a.size * a.dtype.itemsize for a in args)
    return pl.pallas_call(
        kernel,
        out_shape=shapes,
        in_specs=in_specs,
        out_specs=[s for *_, s in outs],
        scratch_shapes=scratch,
        compiler_params=pltpu.CompilerParams(vmem_limit_bytes=mib * 2**20),
        cost_estimate=pl.CostEstimate(flops=flops, bytes_accessed=moved, transcendentals=exps),
    )(*args)


def on_device(queries, key_rows, value_rows):
    full = (TOK, PAIRS * LANES)
    tall = (FOLD * CLASS, LANES)
    spare = (FOLD * CLASS + ROWS, LANES)
    dma = pltpu.SemaphoreType.DMA
    folded = [
        [(g + HALF * half) * INNER + i for half in range(FOLD) for i in range(INNER)]
        for g in range(HALF)
    ]
    halves = [list(range(half * HALF, (half + 1) * HALF)) for half in range(FOLD)]
    own = [
        (pltpu.with_memory_space_constraint(x, pltpu.HBM), HBM)
        for x in (queries, key_rows, value_rows)
    ]
    held = [pltpu.VMEM((3, *full), BF16), dma((3,))]
    (packed,) = call(
        pack_kernel,
        [*own],
        [((FOLD * INNER, CHUNK, LANES), BF16, VMEM)],
        scratch=held,
    )
    got = lax.all_to_all(
        packed, ("outer", "inner"), 0, 0, tiled=True, axis_index_groups=folded
    )
    (far_kv,) = call(
        pick_kernel,
        [(got, VMEM)],
        [((HALF, FOLD * FAR, LANES), BF16, HBM)],
        scratch=[pltpu.VMEM((FOLD * FAR, LANES), BF16), dma((FOLD * HALF,))],
    )
    all_kv = lax.all_to_all(far_kv, "outer", 0, 0, tiled=True, axis_index_groups=halves)
    far_q, state, base, near_out, near_lse = call(
        mid_kernel,
        [(got, VMEM), *own],
        [
            ((FOLD * FAR, LANES), BF16, VMEM),
            (spare, F32, VMEM),
            (tall, F32, VMEM),
            (full, F32, VMEM),
            (full, F32, VMEM),
        ],
        flops=4 * 2 * 512 * 512 * 128,
        exps=2 * 512 * 512,
        scratch=held,
    )
    (back,) = call(
        far_kernel,
        [(far_q, VMEM), (all_kv, VMEM), (state, VMEM), (base, VMEM)],
        [((FOLD * INNER, EIGHT // 2 + 1, 2, LANES), BF16, VMEM)],
        flops=4 * 3 * 128 * 1024 * 128,
        exps=3 * 128 * 1024,
        scratch=[pltpu.VMEM(spare, F32)],
    )
    home = lax.all_to_all(
        back, ("outer", "inner"), 0, 0, tiled=True, axis_index_groups=folded
    )
    (out,) = call(
        home_kernel,
        [(home, VMEM), (near_out, VMEM), (near_lse, VMEM)],
        [(full, F32, HBM)],
        scratch=[pltpu.VMEM(full, F32), dma((PAIRS,))],
    )
    return out


def solution(mesh):
    rows = P(("outer", "inner"), None)
    return jax.shard_map(
        on_device, mesh=mesh, in_specs=(rows,) * 3, out_specs=rows, check_vma=False
    )
```

```python
import jax
import jax.numpy as jnp
from jax import lax
from jax.experimental import pallas as pl
from jax.experimental.pallas import tpu as pltpu
from jax.sharding import PartitionSpec as P

TOK = 64
WIDTH = 64
LANES = 2 * WIDTH
PAIRS = 8
RES = 4
ROWS = TOK // RES
EIGHT = ROWS // 2
INNER = PAIRS * RES
HALF = 8
FOLD = 2
CHUNK = ROWS + EIGHT
CLASS = ROWS * INNER
FAR = CLASS // 4
FLOOR = -1e30
F32 = jnp.float32
BF16 = jnp.bfloat16


def dot(a, b):
    return jnp.dot(a, b, preferred_element_type=F32)


def dot_t(a, b):
    return lax.dot_general(a, b, (((1,), (1,)), ((), ())), preferred_element_type=F32)


def iota(shape, dim):
    return lax.broadcasted_iota(jnp.int32, shape, dim)


def one_hot(shape, row_of, col_of):
    return (row_of(iota(shape, 0)) == col_of(iota(shape, 1))).astype(F32).astype(BF16)


def by_class(r):
    return RES * (r % ROWS) + r // ROWS


def by_half(r):
    return RES * (r // (TOK // 2) * EIGHT + r % EIGHT) + r // EIGHT % RES


def left(shape):
    return iota(shape, len(shape) - 1) < WIDTH


def swap(x):
    return pltpu.roll(x, WIDTH, x.ndim - 1)


def beside(a, b):
    return jnp.where(left(a.shape), a, swap(b))


def beside_right(a, b):
    return jnp.where(left(a.shape), swap(a), b)


def merge(out, lse, other_out, other_lse):
    top = jnp.maximum(lse, other_lse)
    w, other_w = jnp.exp(lse - top), jnp.exp(other_lse - top)
    total = w + other_w
    return (w * out + other_w * other_out) / total, top + jnp.log(total)


def copies_in(refs, held, sems):
    copies = [
        pltpu.make_async_copy(ref, held.at[at], sems.at[at]) for at, ref in enumerate(refs)
    ]
    for copy in copies:
        copy.start()
    return copies


def pack_kernel(q_ref, k_ref, v_ref, out_ref, held, sems):
    copies = copies_in((k_ref, v_ref, q_ref), held, sems)
    order = one_hot((TOK, TOK), by_class, lambda c: c)
    sorted_rows = []
    for at, copy in enumerate(copies):
        copy.wait()
        sorted_rows.append(dot(order, held[at]))
    for pair in range(PAIRS):
        cols = slice(pair * LANES, (pair + 1) * LANES)
        k, v, q = (x[:, cols] for x in sorted_rows)
        q = q.reshape(RES, ROWS, LANES)
        for head, join in enumerate((beside, beside_right)):
            kv = join(k, v).reshape(RES, ROWS, LANES)
            chunk = jnp.concatenate([kv, join(q[:, :EIGHT], q[:, EIGHT:])], axis=1)
            at = head * INNER + pair * RES
            out_ref[at : at + RES, :, :] = chunk.astype(BF16)


def near_level(q_ref, k_ref, v_ref, out_ref, lse_ref):
    allowed = iota((2 * TOK, TOK), 1) <= iota((2 * TOK, TOK), 0) % TOK
    mine = left((TOK, LANES))
    for pair in range(PAIRS):
        cols = slice(pair * LANES, (pair + 1) * LANES)
        q = q_ref[:, cols] * BF16(WIDTH**-0.5)
        zero = jnp.zeros_like(q)
        q = jnp.concatenate([jnp.where(mine, q, zero), jnp.where(mine, zero, q)], axis=0)
        scores = jnp.where(allowed, dot_t(q, k_ref[:, cols]), FLOOR)
        out, lse = softmax_out(scores, v_ref[:, cols])
        lse = jnp.broadcast_to(lse, out.shape)
        out_ref[:, cols] = jnp.where(mine, out[:TOK], out[TOK:])
        lse_ref[:, cols] = jnp.where(mine, lse[:TOK], lse[TOK:])


def softmax_out(scores, values):
    top = jnp.max(scores, axis=1, keepdims=True)
    weights = jnp.exp(scores - top)
    total = jnp.sum(weights, axis=1, keepdims=True)
    return dot(weights.astype(BF16), values) / total, top + jnp.log(total)


def keys_values(got_ref, group):
    return got_ref[group * INNER : (group + 1) * INNER, :ROWS, :].reshape(CLASS, LANES)


def scaled_queries(got_ref, group):
    packed = got_ref[group * INNER : (group + 1) * INNER, ROWS:, :].astype(F32) * WIDTH**-0.5
    q = jnp.concatenate([packed, swap(packed)], axis=1)
    q = jnp.where(left(q.shape), q, 0.0)
    return q.reshape(CLASS, LANES).astype(BF16)


def partner(group):
    return group ^ (HALF + HALF // 2)


def place():
    outer = lax.axis_index("outer")
    group = jnp.where(outer < HALF, outer, partner(outer))
    return lax.axis_index("inner") // (INNER // 4), group


def far_rows(band):
    return one_hot(
        (FAR, CLASS), lambda r: r % INNER * ROWS + r // INNER * 4 + band, lambda c: c
    )


def far_rank(n):
    return n // FAR * FAR + n % INNER * 4 + n % FAR // INNER


def lse_parts(lse):
    high = lse.astype(BF16).astype(F32)
    middle = (lse - high).astype(BF16).astype(F32)
    which = iota(lse.shape, 1) % WIDTH // 16
    parts = jnp.where(which == 1, middle, jnp.where(which == 2, lse - high - middle, 0.0))
    return jnp.where(which == 0, high, parts)


def own_column(parts):
    keep = iota(parts.shape, 2) % 16 == 2 * iota(parts.shape, 1)
    return jnp.where(keep, parts, 0.0)


def open_chunks(chunks):
    chunks = chunks.astype(F32)
    rows = [chunks[:, at, :, :] for at in range(EIGHT // 2)]
    lse = chunks[:, EIGHT // 2, :1, :]
    rows.append(own_column(jnp.broadcast_to(lse, (lse.shape[0], EIGHT, LANES))))
    return jnp.concatenate(rows, axis=1)


def pick_kernel(got_ref, kv_ref, held, sems):
    pick = far_rows(place()[0])
    sends = []
    for group in range(FOLD):
        rows = pl.ds(group * FAR, FAR)
        held[rows, :] = dot(pick, keys_values(got_ref, group)).astype(BF16)
        for to in range(HALF):
            sends.append(
                pltpu.make_async_copy(
                    held.at[rows], kv_ref.at[to, rows], sems.at[len(sends)]
                )
            )
            sends[-1].start()
    for send in sends:
        send.wait()


def mid_kernel(
    got_ref,
    q_ref,
    k_ref,
    v_ref,
    far_q_ref,
    state_ref,
    base_ref,
    near_out_ref,
    near_lse_ref,
    held,
    sems,
):
    copies = copies_in((q_ref, k_ref, v_ref), held, sems)
    pick = far_rows(place()[0])
    block = 128
    for group in range(FOLD):
        q, kv = scaled_queries(got_ref, group), keys_values(got_ref, group)
        far_q_ref[group * FAR : (group + 1) * FAR, :] = dot(pick, q).astype(BF16)
        for start in range(0, CLASS, block):
            end = start + block
            shape = (block, end)
            allowed = iota(shape, 1) <= start + iota(shape, 0)
            scores = jnp.where(allowed, dot_t(q[start:end], kv[:end]), FLOOR)
            out, lse = softmax_out(scores, kv[:end])
            lse = jnp.broadcast_to(lse, out.shape)
            at = group * CLASS + start
            state_ref[at : at + block, :] = jnp.where(left(out.shape), lse, out)
            packed = []
            for x in (out, lse_parts(lse)):
                x = x.reshape(block // ROWS, ROWS, LANES)
                packed.append(beside_right(x[:, :EIGHT], x[:, EIGHT:]))
            packed = jnp.concatenate([packed[0], own_column(packed[1])], axis=1)
            base_ref[at : at + block, :] = packed.reshape(block, LANES)
    for copy in copies:
        copy.wait()
    near_level(held.at[0], held.at[1], held.at[2], near_out_ref, near_lse_ref)


def far_kernel(q_ref, kv_ref, state_ref, base_ref, back_ref, fresh):
    fresh[: FOLD * CLASS, :] = base_ref[...]
    band, group = place()
    first = kv_ref[:, :FAR, :].reshape(HALF * FAR, LANES)
    second = kv_ref[:, FAR:, :].reshape(HALF * FAR, LANES)
    shape = (FAR, HALF * FAR)
    allowed = far_rank(iota(shape, 1)) <= group * FAR + far_rank(iota(shape, 0))
    over_first = dot_t(q_ref[...], first)
    late_rank = far_rank(iota(shape, 1) ^ (HALF // 2 * FAR))
    allowed_late = late_rank <= (group ^ (HALF // 2)) * FAR + far_rank(iota(shape, 0))
    over_second = jnp.where(allowed_late, dot_t(q_ref[FAR:, :], second), FLOOR)
    early = softmax_out(jnp.where(allowed, over_first[:FAR], FLOOR), first)
    late_first = over_first[FAR:]
    top = jnp.maximum(
        jnp.max(late_first, axis=1, keepdims=True), jnp.max(over_second, axis=1, keepdims=True)
    )
    w_first, w_second = jnp.exp(late_first - top), jnp.exp(over_second - top)
    total = jnp.sum(w_first, axis=1, keepdims=True) + jnp.sum(w_second, axis=1, keepdims=True)
    summed = dot(w_first.astype(BF16), first) + dot(w_second.astype(BF16), second)
    late = (summed / total, top + jnp.log(total))
    for at, (far_out, far_lse) in enumerate((early, late)):
        start = at * CLASS + band
        mid = jnp.concatenate(
            [state_ref[pl.ds(start + 4 * lot, INNER, stride=ROWS), :] for lot in range(4)], axis=0
        )
        out, lse = merge(mid, swap(mid), far_out, jnp.broadcast_to(far_lse, far_out.shape))
        column = iota((INNER, LANES), 1) % 16
        for x, down in ((out, 0), (lse_parts(lse), EIGHT)):
            for lot in range(2):
                upper = x[lot * INNER : (lot + 1) * INNER]
                lower = x[(lot + 2) * INNER : (lot + 3) * INNER]
                rows = beside_right(upper, lower)
                if down:
                    rows = jnp.where(column == 2 * (band + 4 * lot), rows, 0.0)
                fresh[pl.ds(start + down + 4 * lot, INNER, stride=ROWS), :] = rows
    back = fresh[: FOLD * CLASS, :].reshape(FOLD * INNER, ROWS, LANES)
    for at in range(EIGHT // 2):
        back_ref[:, at, :, :] = back[:, 2 * at : 2 * at + 2, :].astype(BF16)
    lse = jnp.sum(back[:, EIGHT:, :], axis=1, keepdims=True).astype(BF16)
    back_ref[:, EIGHT // 2, :, :] = jnp.broadcast_to(lse, (FOLD * INNER, 2, LANES))


def home_kernel(got_ref, near_out_ref, near_lse_ref, out_ref, held, sems):
    order = one_hot((TOK, TOK), lambda r: r, by_half)
    shape = (LANES, LANES)
    row, col = iota(shape, 0), iota(shape, 1)
    gather = (row // WIDTH == col // WIDTH).astype(F32).astype(BF16)
    sends = []
    for pair in range(PAIRS):
        cols = slice(pair * LANES, (pair + 1) * LANES)
        rows = slice(pair * RES, (pair + 1) * RES)
        a = open_chunks(got_ref[rows])
        b = open_chunks(got_ref[INNER + pair * RES : INNER + (pair + 1) * RES])
        both = jnp.concatenate([beside(a, b), beside_right(a, b)], axis=0)
        tall = (TOK, LANES)
        out = dot(order, both[:, :EIGHT, :].reshape(tall).astype(BF16))
        parts = dot(order, both[:, EIGHT:, :].reshape(tall).astype(BF16)).astype(BF16)
        lse = dot(parts, gather)
        held[:, cols] = merge(out, lse, near_out_ref[:, cols], near_lse_ref[:, cols])[0]
        sends.append(
            pltpu.make_async_copy(held.at[:, cols], out_ref.at[:, cols], sems.at[pair])
        )
        sends[-1].start()
    for send in sends:
        send.wait()


HBM = pl.BlockSpec(memory_space=pltpu.HBM)
VMEM = pl.BlockSpec(memory_space=pltpu.VMEM)


def call(kernel, ins, outs, flops=0, exps=0, scratch=(), mib=40):
    args, in_specs = [a for a, _ in ins], [s for _, s in ins]
    shapes = [space.memory_space(s, t) for s, t, space in outs]
    moved = sum(a.size * a.dtype.itemsize for a in args)
    return pl.pallas_call(
        kernel,
        out_shape=shapes,
        in_specs=in_specs,
        out_specs=[s for *_, s in outs],
        scratch_shapes=scratch,
        compiler_params=pltpu.CompilerParams(vmem_limit_bytes=mib * 2**20),
        cost_estimate=pl.CostEstimate(flops=flops, bytes_accessed=moved, transcendentals=exps),
    )(*args)


def on_device(queries, key_rows, value_rows):
    full = (TOK, PAIRS * LANES)
    tall = (FOLD * CLASS, LANES)
    spare = (FOLD * CLASS + ROWS, LANES)
    dma = pltpu.SemaphoreType.DMA
    folded = [
        [shared * INNER + i for shared in (g, partner(g)) for i in range(INNER)]
        for g in range(HALF)
    ]
    halves = [list(range(HALF)), [partner(g) for g in range(HALF)]]
    own = [
        (pltpu.with_memory_space_constraint(x, pltpu.HBM), HBM)
        for x in (queries, key_rows, value_rows)
    ]
    held = [pltpu.VMEM((3, *full), BF16), dma((3,))]
    (packed,) = call(
        pack_kernel,
        [*own],
        [((FOLD * INNER, CHUNK, LANES), BF16, VMEM)],
        scratch=held,
    )
    got = lax.all_to_all(
        packed, ("outer", "inner"), 0, 0, tiled=True, axis_index_groups=folded
    )
    (far_kv,) = call(
        pick_kernel,
        [(got, VMEM)],
        [((HALF, FOLD * FAR, LANES), BF16, HBM)],
        scratch=[pltpu.VMEM((FOLD * FAR, LANES), BF16), dma((FOLD * HALF,))],
    )
    all_kv = lax.all_to_all(far_kv, "outer", 0, 0, tiled=True, axis_index_groups=halves)
    far_q, state, base, near_out, near_lse = call(
        mid_kernel,
        [(got, VMEM), *own],
        [
            ((FOLD * FAR, LANES), BF16, VMEM),
            (spare, F32, VMEM),
            (tall, F32, VMEM),
            (full, F32, VMEM),
            (full, F32, VMEM),
        ],
        flops=4 * 2 * 512 * 512 * 128,
        exps=2 * 512 * 512,
        scratch=held,
    )
    (back,) = call(
        far_kernel,
        [(far_q, VMEM), (all_kv, VMEM), (state, VMEM), (base, VMEM)],
        [((FOLD * INNER, EIGHT // 2 + 1, 2, LANES), BF16, VMEM)],
        flops=4 * 3 * 128 * 1024 * 128,
        exps=3 * 128 * 1024,
        scratch=[pltpu.VMEM(spare, F32)],
    )
    home = lax.all_to_all(
        back, ("outer", "inner"), 0, 0, tiled=True, axis_index_groups=folded
    )
    (out,) = call(
        home_kernel,
        [(home, VMEM), (near_out, VMEM), (near_lse, VMEM)],
        [(full, F32, HBM)],
        scratch=[pltpu.VMEM(full, F32), dma((PAIRS,))],
    )
    return out


def solution(mesh):
    rows = P(("outer", "inner"), None)
    return jax.shard_map(
        on_device, mesh=mesh, in_specs=(rows,) * 3, out_specs=rows, check_vma=False
    )
```

```python
import jax
import jax.numpy as jnp
from jax import lax
from jax.experimental import pallas as pl
from jax.experimental.pallas import tpu as pltpu
from jax.sharding import PartitionSpec as P

TOK = 64
WIDTH = 64
LANES = 2 * WIDTH
PAIRS = 8
RES = 4
ROWS = TOK // RES
EIGHT = ROWS // 2
INNER = PAIRS * RES
HALF = 8
FOLD = 2
CHUNK = ROWS + EIGHT
CLASS = ROWS * INNER
FAR = CLASS // 4
FLOOR = -1e30
F32 = jnp.float32
BF16 = jnp.bfloat16


def dot(a, b):
    return jnp.dot(a, b, preferred_element_type=F32)


def dot_t(a, b):
    return lax.dot_general(a, b, (((1,), (1,)), ((), ())), preferred_element_type=F32)


def iota(shape, dim):
    return lax.broadcasted_iota(jnp.int32, shape, dim)


def one_hot(shape, row_of, col_of):
    rows, cols = row_of(iota((shape[0], 1), 0)), col_of(iota((1, shape[1]), 1))
    return (rows == cols).astype(F32).astype(BF16)


def by_class(r):
    return RES * (r % ROWS) + r // ROWS


def by_half(r):
    return RES * (r // (TOK // 2) * EIGHT + r % EIGHT) + r // EIGHT % RES


def left(shape):
    return iota(shape, len(shape) - 1) < WIDTH


def swap(x):
    return pltpu.roll(x, WIDTH, x.ndim - 1)


def beside(a, b):
    return jnp.where(left(a.shape), a, swap(b))


def beside_right(a, b):
    return jnp.where(left(a.shape), swap(a), b)


def merge(out, lse, other_out, other_lse):
    top = jnp.maximum(lse, other_lse)
    w, other_w = jnp.exp(lse - top), jnp.exp(other_lse - top)
    total = w + other_w
    return (w * out + other_w * other_out) / total, top + jnp.log(total)


def copies_in(refs, held, sems):
    copies = [
        pltpu.make_async_copy(ref, held.at[at], sems.at[at]) for at, ref in enumerate(refs)
    ]
    for copy in copies:
        copy.start()
    return copies


def pack_kernel(q_ref, k_ref, v_ref, out_ref, held, sems):
    copies = copies_in((k_ref, v_ref, q_ref), held, sems)
    order = one_hot((TOK, TOK), by_class, lambda c: c)
    sorted_rows = []
    for at, copy in enumerate(copies):
        copy.wait()
        sorted_rows.append(dot(order, held[at]))
    for pair in range(PAIRS):
        cols = slice(pair * LANES, (pair + 1) * LANES)
        k, v, q = (x[:, cols] for x in sorted_rows)
        q = q.reshape(RES, ROWS, LANES)
        for head, join in enumerate((beside, beside_right)):
            kv = join(k, v).reshape(RES, ROWS, LANES)
            chunk = jnp.concatenate([kv, join(q[:, :EIGHT], q[:, EIGHT:])], axis=1)
            at = head * INNER + pair * RES
            out_ref[at : at + RES, :, :] = chunk.astype(BF16)


def near_level(q_ref, k_ref, v_ref, out_ref, lse_ref):
    allowed = iota((2 * TOK, TOK), 1) <= iota((2 * TOK, TOK), 0) % TOK
    mine = left((TOK, LANES))
    for pair in range(PAIRS):
        cols = slice(pair * LANES, (pair + 1) * LANES)
        q = q_ref[:, cols] * BF16(WIDTH**-0.5)
        zero = jnp.zeros_like(q)
        q = jnp.concatenate([jnp.where(mine, q, zero), jnp.where(mine, zero, q)], axis=0)
        scores = jnp.where(allowed, dot_t(q, k_ref[:, cols]), FLOOR)
        out, lse = softmax_out(scores, v_ref[:, cols])
        lse = jnp.broadcast_to(lse, out.shape)
        out_ref[:, cols] = jnp.where(mine, out[:TOK], out[TOK:])
        lse_ref[:, cols] = jnp.where(mine, lse[:TOK], lse[TOK:])


def softmax_out(scores, values):
    top = jnp.max(scores, axis=1, keepdims=True)
    weights = jnp.exp(scores - top)
    total = jnp.sum(weights, axis=1, keepdims=True)
    return dot(weights.astype(BF16), values) / total, top + jnp.log(total)


def keys_values(got_ref, group):
    return got_ref[group * INNER : (group + 1) * INNER, :ROWS, :].reshape(CLASS, LANES)


def scaled_queries(got_ref, group):
    packed = got_ref[group * INNER : (group + 1) * INNER, ROWS:, :].astype(F32) * WIDTH**-0.5
    q = jnp.concatenate([packed, swap(packed)], axis=1)
    q = jnp.where(left(q.shape), q, 0.0)
    return q.reshape(CLASS, LANES).astype(BF16)


def partner(group):
    return group ^ (HALF + HALF // 2)


def place():
    outer = lax.axis_index("outer")
    group = jnp.where(outer < HALF, outer, partner(outer))
    return lax.axis_index("inner") // (INNER // 4), group


def far_rows(band):
    return one_hot(
        (FAR, CLASS), lambda r: r % INNER * ROWS + r // INNER * 4 + band, lambda c: c
    )


def far_rank(n):
    return n // FAR * FAR + n % INNER * 4 + n % FAR // INNER


def lse_parts(lse):
    high = lse.astype(BF16).astype(F32)
    middle = (lse - high).astype(BF16).astype(F32)
    which = iota(lse.shape, 1) % WIDTH // 16
    parts = jnp.where(which == 1, middle, jnp.where(which == 2, lse - high - middle, 0.0))
    return jnp.where(which == 0, high, parts)


def own_column(parts):
    keep = iota(parts.shape, 2) % 16 == 2 * iota(parts.shape, 1)
    return jnp.where(keep, parts, 0.0)


def open_chunks(chunks):
    chunks = chunks.astype(F32)
    rows = [chunks[:, at, :, :] for at in range(EIGHT // 2)]
    lse = chunks[:, EIGHT // 2, :1, :]
    rows.append(own_column(jnp.broadcast_to(lse, (lse.shape[0], EIGHT, LANES))))
    return jnp.concatenate(rows, axis=1)


def pick_kernel(got_ref, kv_ref, held, sems):
    pick = far_rows(place()[0])
    sends = []
    for group in range(FOLD):
        rows = pl.ds(group * FAR, FAR)
        held[rows, :] = dot(pick, keys_values(got_ref, group)).astype(BF16)
        for to in range(HALF):
            sends.append(
                pltpu.make_async_copy(
                    held.at[rows], kv_ref.at[to, rows], sems.at[len(sends)]
                )
            )
            sends[-1].start()
    for send in sends:
        send.wait()


def mid_kernel(
    got_ref,
    q_ref,
    k_ref,
    v_ref,
    far_q_ref,
    state_ref,
    base_ref,
    near_out_ref,
    near_lse_ref,
    held,
    sems,
):
    copies = copies_in((q_ref, k_ref, v_ref), held, sems)
    pick = far_rows(place()[0])
    block = 128
    for group in range(FOLD):
        q, kv = scaled_queries(got_ref, group), keys_values(got_ref, group)
        far_q_ref[group * FAR : (group + 1) * FAR, :] = dot(pick, q).astype(BF16)
        for start in range(0, CLASS, block):
            end = start + block
            shape = (block, end)
            allowed = iota(shape, 1) <= start + iota(shape, 0)
            scores = jnp.where(allowed, dot_t(q[start:end], kv[:end]), FLOOR)
            out, lse = softmax_out(scores, kv[:end])
            lse = jnp.broadcast_to(lse, out.shape)
            at = group * CLASS + start
            state_ref[at : at + block, :] = jnp.where(left(out.shape), lse, out)
            packed = []
            for x in (out, lse_parts(lse)):
                x = x.reshape(block // ROWS, ROWS, LANES)
                packed.append(beside_right(x[:, :EIGHT], x[:, EIGHT:]))
            packed = jnp.concatenate([packed[0], own_column(packed[1])], axis=1)
            base_ref[at : at + block, :] = packed.reshape(block, LANES)
    for copy in copies:
        copy.wait()
    near_level(held.at[0], held.at[1], held.at[2], near_out_ref, near_lse_ref)


def far_kernel(q_ref, kv_ref, state_ref, base_ref, back_ref, fresh):
    fresh[: FOLD * CLASS, :] = base_ref[...]
    band, group = place()
    first = kv_ref[:, :FAR, :].reshape(HALF * FAR, LANES)
    second = kv_ref[:, FAR:, :].reshape(HALF * FAR, LANES)
    keys, mine = iota((1, HALF * FAR), 1), far_rank(iota((FAR, 1), 0))
    allowed = far_rank(keys) <= group * FAR + mine
    over_first = dot_t(q_ref[...], first)
    late_rank = far_rank(keys ^ (HALF // 2 * FAR))
    allowed_late = late_rank <= (group ^ (HALF // 2)) * FAR + mine
    over_second = jnp.where(allowed_late, dot_t(q_ref[FAR:, :], second), FLOOR)
    early = softmax_out(jnp.where(allowed, over_first[:FAR], FLOOR), first)
    late_first = over_first[FAR:]
    top = jnp.maximum(
        jnp.max(late_first, axis=1, keepdims=True), jnp.max(over_second, axis=1, keepdims=True)
    )
    w_first, w_second = jnp.exp(late_first - top), jnp.exp(over_second - top)
    total = jnp.sum(w_first, axis=1, keepdims=True) + jnp.sum(w_second, axis=1, keepdims=True)
    summed = dot(w_first.astype(BF16), first) + dot(w_second.astype(BF16), second)
    late = (summed / total, top + jnp.log(total))
    for at, (far_out, far_lse) in enumerate((early, late)):
        start = at * CLASS + band
        mid = jnp.concatenate(
            [state_ref[pl.ds(start + 4 * lot, INNER, stride=ROWS), :] for lot in range(4)], axis=0
        )
        out, lse = merge(mid, swap(mid), far_out, jnp.broadcast_to(far_lse, far_out.shape))
        column = iota((INNER, LANES), 1) % 16
        for x, down in ((out, 0), (lse_parts(lse), EIGHT)):
            for lot in range(2):
                upper = x[lot * INNER : (lot + 1) * INNER]
                lower = x[(lot + 2) * INNER : (lot + 3) * INNER]
                rows = beside_right(upper, lower)
                if down:
                    rows = jnp.where(column == 2 * (band + 4 * lot), rows, 0.0)
                fresh[pl.ds(start + down + 4 * lot, INNER, stride=ROWS), :] = rows
    back = fresh[: FOLD * CLASS, :].reshape(FOLD * INNER, ROWS, LANES)
    for at in range(EIGHT // 2):
        back_ref[:, at, :, :] = back[:, 2 * at : 2 * at + 2, :].astype(BF16)
    lse = jnp.sum(back[:, EIGHT:, :], axis=1, keepdims=True).astype(BF16)
    back_ref[:, EIGHT // 2, :, :] = jnp.broadcast_to(lse, (FOLD * INNER, 2, LANES))


def home_kernel(got_ref, near_out_ref, near_lse_ref, out_ref, held, sems):
    order = one_hot((TOK, TOK), lambda r: r, by_half)
    shape = (LANES, LANES)
    row, col = iota(shape, 0), iota(shape, 1)
    gather = (row // WIDTH == col // WIDTH).astype(F32).astype(BF16)
    sends = []
    for pair in range(PAIRS):
        cols = slice(pair * LANES, (pair + 1) * LANES)
        rows = slice(pair * RES, (pair + 1) * RES)
        a = open_chunks(got_ref[rows])
        b = open_chunks(got_ref[INNER + pair * RES : INNER + (pair + 1) * RES])
        both = jnp.concatenate([beside(a, b), beside_right(a, b)], axis=0)
        tall = (TOK, LANES)
        out = dot(order, both[:, :EIGHT, :].reshape(tall).astype(BF16))
        parts = dot(order, both[:, EIGHT:, :].reshape(tall).astype(BF16)).astype(BF16)
        lse = dot(parts, gather)
        held[:, cols] = merge(out, lse, near_out_ref[:, cols], near_lse_ref[:, cols])[0]
        sends.append(
            pltpu.make_async_copy(held.at[:, cols], out_ref.at[:, cols], sems.at[pair])
        )
        sends[-1].start()
    for send in sends:
        send.wait()


HBM = pl.BlockSpec(memory_space=pltpu.HBM)
VMEM = pl.BlockSpec(memory_space=pltpu.VMEM)


def call(kernel, ins, outs, flops=0, exps=0, scratch=(), mib=40):
    args, in_specs = [a for a, _ in ins], [s for _, s in ins]
    shapes = [space.memory_space(s, t) for s, t, space in outs]
    moved = sum(a.size * a.dtype.itemsize for a in args)
    return pl.pallas_call(
        kernel,
        out_shape=shapes,
        in_specs=in_specs,
        out_specs=[s for *_, s in outs],
        scratch_shapes=scratch,
        compiler_params=pltpu.CompilerParams(vmem_limit_bytes=mib * 2**20),
        cost_estimate=pl.CostEstimate(flops=flops, bytes_accessed=moved, transcendentals=exps),
    )(*args)


def on_device(queries, key_rows, value_rows):
    full = (TOK, PAIRS * LANES)
    tall = (FOLD * CLASS, LANES)
    spare = (FOLD * CLASS + ROWS, LANES)
    dma = pltpu.SemaphoreType.DMA
    folded = [
        [shared * INNER + i for shared in (g, partner(g)) for i in range(INNER)]
        for g in range(HALF)
    ]
    halves = [list(range(HALF)), [partner(g) for g in range(HALF)]]
    own = [
        (pltpu.with_memory_space_constraint(x, pltpu.HBM), HBM)
        for x in (queries, key_rows, value_rows)
    ]
    held = [pltpu.VMEM((3, *full), BF16), dma((3,))]
    (packed,) = call(
        pack_kernel,
        [*own],
        [((FOLD * INNER, CHUNK, LANES), BF16, VMEM)],
        scratch=held,
    )
    got = lax.all_to_all(
        packed, ("outer", "inner"), 0, 0, tiled=True, axis_index_groups=folded
    )
    (far_kv,) = call(
        pick_kernel,
        [(got, VMEM)],
        [((HALF, FOLD * FAR, LANES), BF16, HBM)],
        scratch=[pltpu.VMEM((FOLD * FAR, LANES), BF16), dma((FOLD * HALF,))],
    )
    all_kv = lax.all_to_all(far_kv, "outer", 0, 0, tiled=True, axis_index_groups=halves)
    far_q, state, base, near_out, near_lse = call(
        mid_kernel,
        [(got, VMEM), *own],
        [
            ((FOLD * FAR, LANES), BF16, VMEM),
            (spare, F32, VMEM),
            (tall, F32, VMEM),
            (full, F32, VMEM),
            (full, F32, VMEM),
        ],
        flops=4 * 2 * 512 * 512 * 128,
        exps=2 * 512 * 512,
        scratch=held,
    )
    (back,) = call(
        far_kernel,
        [(far_q, VMEM), (all_kv, VMEM), (state, VMEM), (base, VMEM)],
        [((FOLD * INNER, EIGHT // 2 + 1, 2, LANES), BF16, VMEM)],
        flops=4 * 3 * 128 * 1024 * 128,
        exps=3 * 128 * 1024,
        scratch=[pltpu.VMEM(spare, F32)],
    )
    home = lax.all_to_all(
        back, ("outer", "inner"), 0, 0, tiled=True, axis_index_groups=folded
    )
    (out,) = call(
        home_kernel,
        [(home, VMEM), (near_out, VMEM), (near_lse, VMEM)],
        [(full, F32, HBM)],
        scratch=[pltpu.VMEM(full, F32), dma((PAIRS,))],
    )
    return out


def solution(mesh):
    rows = P(("outer", "inner"), None)
    return jax.shard_map(
        on_device, mesh=mesh, in_specs=(rows,) * 3, out_specs=rows, check_vma=False
    )
```

```python
import jax
import jax.numpy as jnp
from jax import lax
from jax.experimental import pallas as pl
from jax.experimental.pallas import tpu as pltpu
from jax.sharding import PartitionSpec as P

TOK = 64
WIDTH = 64
LANES = 2 * WIDTH
PAIRS = 8
RES = 4
ROWS = TOK // RES
EIGHT = ROWS // 2
INNER = PAIRS * RES
HALF = 8
FOLD = 2
CHUNK = ROWS + EIGHT
CLASS = ROWS * INNER
FAR = CLASS // 4
FLOOR = -1e30
F32 = jnp.float32
BF16 = jnp.bfloat16


def dot(a, b):
    return jnp.dot(a, b, preferred_element_type=F32)


def dot_t(a, b):
    return lax.dot_general(a, b, (((1,), (1,)), ((), ())), preferred_element_type=F32)


def iota(shape, dim):
    return lax.broadcasted_iota(jnp.int32, shape, dim)


def one_hot(shape, row_of, col_of):
    rows, cols = row_of(iota((shape[0], 1), 0)), col_of(iota((1, shape[1]), 1))
    return (rows == cols).astype(F32).astype(BF16)


def by_class(r):
    return RES * (r % ROWS) + r // ROWS


def by_half(r):
    return RES * (r // (TOK // 2) * EIGHT + r % EIGHT) + r // EIGHT % RES


def left(shape):
    return iota(shape, len(shape) - 1) < WIDTH


def swap(x):
    return pltpu.roll(x, WIDTH, x.ndim - 1)


def beside(a, b):
    return jnp.where(left(a.shape), a, swap(b))


def beside_right(a, b):
    return jnp.where(left(a.shape), swap(a), b)


def merge(out, lse, other_out, other_lse):
    top = jnp.maximum(lse, other_lse)
    w, other_w = jnp.exp(lse - top), jnp.exp(other_lse - top)
    total = w + other_w
    return (w * out + other_w * other_out) / total, top + jnp.log(total)


def copies_in(refs, held, sems):
    copies = [
        pltpu.make_async_copy(ref, held.at[at], sems.at[at]) for at, ref in enumerate(refs)
    ]
    for copy in copies:
        copy.start()
    return copies


def pack_kernel(q_ref, k_ref, v_ref, out_ref, held, sems):
    copies = copies_in((k_ref, v_ref, q_ref), held, sems)
    order = one_hot((TOK, TOK), by_class, lambda c: c)
    sorted_rows = []
    for at, copy in enumerate(copies):
        copy.wait()
        sorted_rows.append(dot(order, held[at]))
    for pair in range(PAIRS):
        cols = slice(pair * LANES, (pair + 1) * LANES)
        k, v, q = (x[:, cols] for x in sorted_rows)
        q = q.reshape(RES, ROWS, LANES)
        for head, join in enumerate((beside, beside_right)):
            kv = join(k, v).reshape(RES, ROWS, LANES)
            chunk = jnp.concatenate([kv, join(q[:, :EIGHT], q[:, EIGHT:])], axis=1)
            at = head * INNER + pair * RES
            out_ref[at : at + RES, :, :] = chunk.astype(BF16)


def near_level(q_ref, k_ref, v_ref, out_ref, lse_ref):
    allowed = iota((2 * TOK, TOK), 1) <= iota((2 * TOK, TOK), 0) % TOK
    mine = left((TOK, LANES))
    for pair in range(PAIRS):
        cols = slice(pair * LANES, (pair + 1) * LANES)
        q = q_ref[:, cols] * BF16(WIDTH**-0.5)
        zero = jnp.zeros_like(q)
        q = jnp.concatenate([jnp.where(mine, q, zero), jnp.where(mine, zero, q)], axis=0)
        scores = jnp.where(allowed, dot_t(q, k_ref[:, cols]), FLOOR)
        out, lse = softmax_out(scores, v_ref[:, cols])
        lse = jnp.broadcast_to(lse, out.shape)
        out_ref[:, cols] = jnp.where(mine, out[:TOK], out[TOK:])
        lse_ref[:, cols] = jnp.where(mine, lse[:TOK], lse[TOK:])


def softmax_out(scores, values):
    top = jnp.max(scores, axis=1, keepdims=True)
    weights = jnp.exp(scores - top)
    total = jnp.sum(weights, axis=1, keepdims=True)
    return dot(weights.astype(BF16), values) / total, top + jnp.log(total)


def keys_values(got_ref, group):
    return got_ref[group * INNER : (group + 1) * INNER, :ROWS, :].reshape(CLASS, LANES)


def scaled_queries(got_ref, group):
    packed = got_ref[group * INNER : (group + 1) * INNER, ROWS:, :].astype(F32) * WIDTH**-0.5
    q = jnp.concatenate([packed, swap(packed)], axis=1)
    q = jnp.where(left(q.shape), q, 0.0)
    return q.reshape(CLASS, LANES).astype(BF16)


def partner(group):
    return group ^ (HALF + HALF // 2)


def place():
    outer = lax.axis_index("outer")
    group = jnp.where(outer < HALF, outer, partner(outer))
    return lax.axis_index("inner") // (INNER // 4), group


def far_rows(band):
    return one_hot(
        (FAR, CLASS), lambda r: r % INNER * ROWS + r // INNER * 4 + band, lambda c: c
    )


def far_rank(n):
    return n // FAR * FAR + n % INNER * 4 + n % FAR // INNER


def lse_parts(lse):
    high = lse.astype(BF16).astype(F32)
    middle = (lse - high).astype(BF16).astype(F32)
    which = iota(lse.shape, 1) % WIDTH // 16
    parts = jnp.where(which == 1, middle, jnp.where(which == 2, lse - high - middle, 0.0))
    return jnp.where(which == 0, high, parts)


def own_column(parts):
    keep = iota(parts.shape, 2) % 16 == 2 * iota(parts.shape, 1)
    return jnp.where(keep, parts, 0.0)


def open_chunks(chunks):
    chunks = chunks.astype(F32)
    rows = [chunks[:, at, :, :] for at in range(EIGHT // 2)]
    lse = chunks[:, EIGHT // 2, :1, :]
    rows.append(own_column(jnp.broadcast_to(lse, (lse.shape[0], EIGHT, LANES))))
    return jnp.concatenate(rows, axis=1)


def pick_kernel(got_ref, kv_ref, held, sems):
    pick = far_rows(place()[0])
    sends = []
    for group in range(FOLD):
        rows = pl.ds(group * FAR, FAR)
        held[rows, :] = dot(pick, keys_values(got_ref, group)).astype(BF16)
        for to in range(HALF):
            sends.append(
                pltpu.make_async_copy(
                    held.at[rows], kv_ref.at[to, rows], sems.at[len(sends)]
                )
            )
            sends[-1].start()
    for send in sends:
        send.wait()


def mid_kernel(
    got_ref,
    q_ref,
    k_ref,
    v_ref,
    far_q_ref,
    far_mid_ref,
    base_ref,
    near_out_ref,
    near_lse_ref,
    held,
    sems,
    state_ref,
):
    copies = copies_in((q_ref, k_ref, v_ref), held, sems)
    pick = far_rows(place()[0])
    block = 128
    for group in range(FOLD):
        q, kv = scaled_queries(got_ref, group), keys_values(got_ref, group)
        far_q_ref[group * FAR : (group + 1) * FAR, :] = dot(pick, q).astype(BF16)
        for start in range(0, CLASS, block):
            end = start + block
            shape = (block, end)
            allowed = iota(shape, 1) <= start + iota(shape, 0)
            scores = jnp.where(allowed, dot_t(q[start:end], kv[:end]), FLOOR)
            out, lse = softmax_out(scores, kv[:end])
            lse = jnp.broadcast_to(lse, out.shape)
            at = group * CLASS + start
            state_ref[at : at + block, :] = jnp.where(left(out.shape), lse, out)
            packed = []
            for x in (out, lse_parts(lse)):
                x = x.reshape(block // ROWS, ROWS, LANES)
                packed.append(beside_right(x[:, :EIGHT], x[:, EIGHT:]))
            packed = jnp.concatenate([packed[0], own_column(packed[1])], axis=1)
            base_ref[at : at + block, :] = packed.reshape(block, LANES)
    for at in range(FOLD):
        for lot in range(4):
            rows = pl.ds(at * CLASS + place()[0] + 4 * lot, INNER, stride=ROWS)
            to = at * FAR + lot * INNER
            far_mid_ref[to : to + INNER, :] = state_ref[rows, :]
    for copy in copies:
        copy.wait()
    near_level(held.at[0], held.at[1], held.at[2], near_out_ref, near_lse_ref)


def far_kernel(q_ref, kv_ref, far_mid_ref, base_ref, back_ref, fresh):
    fresh[: FOLD * CLASS, :] = base_ref[...]
    band, group = place()
    first = kv_ref[:, :FAR, :].reshape(HALF * FAR, LANES)
    second = kv_ref[:, FAR:, :].reshape(HALF * FAR, LANES)
    keys, mine = iota((1, HALF * FAR), 1), far_rank(iota((FAR, 1), 0))
    allowed = far_rank(keys) <= group * FAR + mine
    over_first = dot_t(q_ref[...], first)
    late_rank = far_rank(keys ^ (HALF // 2 * FAR))
    allowed_late = late_rank <= (group ^ (HALF // 2)) * FAR + mine
    over_second = jnp.where(allowed_late, dot_t(q_ref[FAR:, :], second), FLOOR)
    early = softmax_out(jnp.where(allowed, over_first[:FAR], FLOOR), first)
    late_first = over_first[FAR:]
    top = jnp.maximum(
        jnp.max(late_first, axis=1, keepdims=True), jnp.max(over_second, axis=1, keepdims=True)
    )
    w_first, w_second = jnp.exp(late_first - top), jnp.exp(over_second - top)
    total = jnp.sum(w_first, axis=1, keepdims=True) + jnp.sum(w_second, axis=1, keepdims=True)
    summed = dot(w_first.astype(BF16), first) + dot(w_second.astype(BF16), second)
    late = (summed / total, top + jnp.log(total))
    for at, (far_out, far_lse) in enumerate((early, late)):
        start = at * CLASS + band
        mid = far_mid_ref[at * FAR : (at + 1) * FAR, :]
        out, lse = merge(mid, swap(mid), far_out, jnp.broadcast_to(far_lse, far_out.shape))
        column = iota((INNER, LANES), 1) % 16
        for x, down in ((out, 0), (lse_parts(lse), EIGHT)):
            for lot in range(2):
                upper = x[lot * INNER : (lot + 1) * INNER]
                lower = x[(lot + 2) * INNER : (lot + 3) * INNER]
                rows = beside_right(upper, lower)
                if down:
                    rows = jnp.where(column == 2 * (band + 4 * lot), rows, 0.0)
                fresh[pl.ds(start + down + 4 * lot, INNER, stride=ROWS), :] = rows
    back = fresh[: FOLD * CLASS, :].reshape(FOLD * INNER, ROWS, LANES)
    for at in range(EIGHT // 2):
        back_ref[:, at, :, :] = back[:, 2 * at : 2 * at + 2, :].astype(BF16)
    lse = jnp.sum(back[:, EIGHT:, :], axis=1, keepdims=True).astype(BF16)
    back_ref[:, EIGHT // 2, :, :] = jnp.broadcast_to(lse, (FOLD * INNER, 2, LANES))


def home_kernel(got_ref, near_out_ref, near_lse_ref, out_ref, held, sems):
    order = one_hot((TOK, TOK), lambda r: r, by_half)
    shape = (LANES, LANES)
    row, col = iota(shape, 0), iota(shape, 1)
    gather = (row // WIDTH == col // WIDTH).astype(F32).astype(BF16)
    sends = []
    for pair in range(PAIRS):
        cols = slice(pair * LANES, (pair + 1) * LANES)
        rows = slice(pair * RES, (pair + 1) * RES)
        a = open_chunks(got_ref[rows])
        b = open_chunks(got_ref[INNER + pair * RES : INNER + (pair + 1) * RES])
        both = jnp.concatenate([beside(a, b), beside_right(a, b)], axis=0)
        tall = (TOK, LANES)
        out = dot(order, both[:, :EIGHT, :].reshape(tall).astype(BF16))
        parts = dot(order, both[:, EIGHT:, :].reshape(tall).astype(BF16)).astype(BF16)
        lse = dot(parts, gather)
        held[:, cols] = merge(out, lse, near_out_ref[:, cols], near_lse_ref[:, cols])[0]
        sends.append(
            pltpu.make_async_copy(held.at[:, cols], out_ref.at[:, cols], sems.at[pair])
        )
        sends[-1].start()
    for send in sends:
        send.wait()


HBM = pl.BlockSpec(memory_space=pltpu.HBM)
VMEM = pl.BlockSpec(memory_space=pltpu.VMEM)


def call(kernel, ins, outs, flops=0, exps=0, scratch=(), mib=40):
    args, in_specs = [a for a, _ in ins], [s for _, s in ins]
    shapes = [space.memory_space(s, t) for s, t, space in outs]
    moved = sum(a.size * a.dtype.itemsize for a in args)
    return pl.pallas_call(
        kernel,
        out_shape=shapes,
        in_specs=in_specs,
        out_specs=[s for *_, s in outs],
        scratch_shapes=scratch,
        compiler_params=pltpu.CompilerParams(vmem_limit_bytes=mib * 2**20),
        cost_estimate=pl.CostEstimate(flops=flops, bytes_accessed=moved, transcendentals=exps),
    )(*args)


def on_device(queries, key_rows, value_rows):
    full = (TOK, PAIRS * LANES)
    tall = (FOLD * CLASS, LANES)
    spare = (FOLD * CLASS + ROWS, LANES)
    dma = pltpu.SemaphoreType.DMA
    folded = [
        [shared * INNER + i for shared in (g, partner(g)) for i in range(INNER)]
        for g in range(HALF)
    ]
    halves = [list(range(HALF)), [partner(g) for g in range(HALF)]]
    own = [
        (pltpu.with_memory_space_constraint(x, pltpu.HBM), HBM)
        for x in (queries, key_rows, value_rows)
    ]
    held = [pltpu.VMEM((3, *full), BF16), dma((3,))]
    (packed,) = call(
        pack_kernel,
        [*own],
        [((FOLD * INNER, CHUNK, LANES), BF16, VMEM)],
        scratch=held,
    )
    got = lax.all_to_all(
        packed, ("outer", "inner"), 0, 0, tiled=True, axis_index_groups=folded
    )
    (far_kv,) = call(
        pick_kernel,
        [(got, VMEM)],
        [((HALF, FOLD * FAR, LANES), BF16, HBM)],
        scratch=[pltpu.VMEM((FOLD * FAR, LANES), BF16), dma((FOLD * HALF,))],
    )
    all_kv = lax.all_to_all(far_kv, "outer", 0, 0, tiled=True, axis_index_groups=halves)
    far_q, state, base, near_out, near_lse = call(
        mid_kernel,
        [(got, VMEM), *own],
        [
            ((FOLD * FAR, LANES), BF16, VMEM),
            ((FOLD * FAR, LANES), F32, VMEM),
            (tall, F32, VMEM),
            (full, F32, VMEM),
            (full, F32, VMEM),
        ],
        flops=4 * 2 * 512 * 512 * 128,
        exps=2 * 512 * 512,
        scratch=[*held, pltpu.VMEM(spare, F32)],
    )
    (back,) = call(
        far_kernel,
        [(far_q, VMEM), (all_kv, VMEM), (state, VMEM), (base, VMEM)],
        [((FOLD * INNER, EIGHT // 2 + 1, 2, LANES), BF16, VMEM)],
        flops=4 * 3 * 128 * 1024 * 128,
        exps=3 * 128 * 1024,
        scratch=[pltpu.VMEM(spare, F32)],
    )
    home = lax.all_to_all(
        back, ("outer", "inner"), 0, 0, tiled=True, axis_index_groups=folded
    )
    (out,) = call(
        home_kernel,
        [(home, VMEM), (near_out, VMEM), (near_lse, VMEM)],
        [(full, F32, HBM)],
        scratch=[pltpu.VMEM(full, F32), dma((PAIRS,))],
    )
    return out


def solution(mesh):
    rows = P(("outer", "inner"), None)
    return jax.shard_map(
        on_device, mesh=mesh, in_specs=(rows,) * 3, out_specs=rows, check_vma=False
    )
```
